128 devices in a mesh: outer: 32 (over x, z, core), inner: 4 (over y).
Axes of the slice: x: 4, y: 4, z: 4, core: 2. Of those that a mesh axis runs over, the one named last changes fastest.
Arguments:
- inputs: bfloat16 [16384, 4096], P(('outer', 'inner')), may hold values from -6 to 6
- log_decay: bfloat16 [16384, 64], P(('outer', 'inner')), may hold values from -1 to 0, as said below
- read_in: bfloat16 [16384, 1024], P(('outer', 'inner')), may hold values from -0.29882812 to 0.29882812
- read_out: bfloat16 [16384, 1024], P(('outer', 'inner')), may hold values from -0.29882812 to 0.29882812
- initial_state: float32 [64, 64, 128], P('inner'), may hold values from -24 to 24
- output_grad: bfloat16 [16384, 4096], P(('outer', 'inner')), may hold values from -6 to 6
Outputs:
- outputs: bfloat16 [16384, 4096], P(('outer', 'inner'))
- inputs_grad: bfloat16 [16384, 4096], P(('outer', 'inner'))
- decay_grad: bfloat16 [16384, 64], P(('outer', 'inner'))
- read_in_grad: bfloat16 [16384, 1024], P(('outer', 'inner'))
- read_out_grad: bfloat16 [16384, 1024], P(('outer', 'inner'))
- initial_grad: float32 [64, 64, 128], P('inner')
The draws below stay inside these ranges and needn't reach their ends.
Inputs may be any that keep to these rules, and one draw needn't show every extreme that they name: log_decay is negative.
All inputs are finite; a program needn't handle non-finite values.
Results may differ from the reference program's by a relative error of at most 0.022.
Values may be sent and summed in bfloat16 or wider, within the bound.
A program may use at most 512 MiB of HBM per device.

```python
import jax
import jax.numpy as jnp
from jax import lax

NUM_ATTENDERS = 64
P_SIZE = 64
N = 128
G = 8
L = 128
TOK_DEV = 128
SEGMENT_STEPS = 16384


def draw_log_decay(key, part):
    key = jax.random.fold_in(key, 7)
    subkeys = jax.random.split(key, 7)
    slow_share = 0.5
    rough = jnp.exp(jax.random.uniform(subkeys[0], (SEGMENT_STEPS, NUM_ATTENDERS), jnp.float32, -0.7, 0.7))
    slow_heads = jax.random.bernoulli(subkeys[1], slow_share, (NUM_ATTENDERS,))
    fast_rate = jnp.exp(jax.random.uniform(subkeys[2], (NUM_ATTENDERS,), jnp.float32, jnp.log(1.0 / 50.0), jnp.log(1.0 / 30.0)))
    slow_rate = jnp.exp(jax.random.uniform(subkeys[3], (NUM_ATTENDERS,), jnp.float32, jnp.log(0.1), jnp.log(0.5))) / SEGMENT_STEPS
    rate = jnp.where(slow_heads, slow_rate, fast_rate)
    device_factor = jnp.exp(jax.random.uniform(subkeys[4], (SEGMENT_STEPS // TOK_DEV, 1, NUM_ATTENDERS), jnp.float32, -0.7, 0.7))
    segment_start = (rough.reshape(SEGMENT_STEPS // TOK_DEV, TOK_DEV, NUM_ATTENDERS) * device_factor).reshape(SEGMENT_STEPS, NUM_ATTENDERS) * rate[None, :]
    sample_locations = jax.random.randint(subkeys[5], (3,), 0, SEGMENT_STEPS)
    objective_terms = jax.random.uniform(subkeys[6], (3, NUM_ATTENDERS), jnp.float32, 0.22, 0.45)
    element_place = lax.broadcasted_iota(jnp.int32, (SEGMENT_STEPS, 1), 0)
    span_extent = jnp.zeros((SEGMENT_STEPS, NUM_ATTENDERS), jnp.float32)
    for chosen_slot in range(3):
        span_extent = span_extent + jnp.where(element_place == sample_locations[chosen_slot], objective_terms[chosen_slot][None, :], 0.0)
    return (-(segment_start + span_extent)).astype(jnp.bfloat16)


def level_of(stream_key, extent, cuts, smallest, largest):
    def one(axis_at, parts):
        draws = jax.random.uniform(jax.random.fold_in(jax.random.fold_in(stream_key, 6), axis_at), (parts,), jnp.float32, smallest / len(cuts), largest / len(cuts))
        return jnp.repeat(jnp.exp(draws), extent[axis_at] // parts).reshape((-1,) + (1,) * (len(extent) - axis_at - 1))

    gain = one(*cuts[0])
    for cut in cuts[1:]:
        gain = gain * one(*cut)
    return gain


def centred(key, dims, scale, bound, cuts=(), kind=jnp.bfloat16):
    factor_of = level_of(key, dims, cuts, -0.22, 0.18) if cuts else 1.0
    entries = jax.random.normal(key, dims, jnp.float32) * scale * factor_of
    return jnp.minimum(jnp.maximum(entries, -bound), bound).astype(kind)


def setup_inputs(seed: int = 0) -> dict:
    key_list = jax.random.split(jax.random.key(seed), 7)
    inputs = centred(key_list[0], (SEGMENT_STEPS, NUM_ATTENDERS * P_SIZE), 1.0, 6.0, ((0, 128),))
    log_decay = draw_log_decay(jax.random.fold_in(key_list[6], 71), 0)
    read_in = centred(key_list[2], (SEGMENT_STEPS, G * N), 0.05, 0.29882812, ((0, 128),))
    read_out = centred(key_list[3], (SEGMENT_STEPS, G * N), 0.05, 0.29882812, ((0, 128),))
    initial_state = centred(key_list[4], (NUM_ATTENDERS, P_SIZE, N), 4.0, 24.0, ((0, 4),), jnp.float32)
    output_grad = centred(key_list[5], (SEGMENT_STEPS, NUM_ATTENDERS * P_SIZE), 1.0, 6.0, ((0, 128),))
    return dict(inputs=inputs, log_decay=log_decay, read_in=read_in, read_out=read_out, initial_state=initial_state, output_grad=output_grad)


def block_advance(state, pieces):
    piece_x, piece_decay, piece_in, piece_out = pieces
    heads = state.shape[0]
    width = state.shape[1]
    depth = state.shape[2]
    length = piece_x.shape[0]
    groups = piece_in.shape[1] // depth
    ratio = heads // groups
    summed = jnp.cumsum(piece_decay.astype(jnp.float32), axis=0)
    row_index = lax.broadcasted_iota(jnp.int32, (length, length), 0)
    col_index = lax.broadcasted_iota(jnp.int32, (length, length), 1)
    causal = (row_index >= col_index)[None]
    spread = summed.T[:, :, None] - summed.T[:, None, :]
    decays = jnp.where(causal, jnp.exp(jnp.where(causal, spread, 0.0)), 0.0)
    in_rows = piece_in.reshape(length, groups, depth)
    out_rows = piece_out.reshape(length, groups, depth)
    input_rows = piece_x.reshape(length, groups, ratio, width)
    scores = jnp.einsum('tgn,sgn->gts', out_rows, in_rows, preferred_element_type=jnp.float32)
    weight_factors = (scores[:, None] * decays.reshape(groups, ratio, length, length)).astype(jnp.bfloat16)
    local_portion = jnp.einsum('zkjm,mzkl->jzkl', weight_factors, input_rows, preferred_element_type=jnp.float32)
    state_low = state.astype(jnp.bfloat16).reshape(groups, ratio, width, depth)
    carried = jnp.einsum('tgn,grpn->tgrp', out_rows, state_low, preferred_element_type=jnp.float32)
    carried = carried * jnp.exp(summed).reshape(length, groups, ratio)[..., None]
    result = (local_portion + carried).reshape(length, heads * width).astype(jnp.bfloat16)
    to_end = jnp.exp(summed[-1:] - summed).reshape(length, groups, ratio)[..., None]
    weighted = (input_rows * to_end).astype(jnp.bfloat16)
    gained = jnp.einsum('tgrp,tgn->grpn', weighted, in_rows, preferred_element_type=jnp.float32)
    advanced = jnp.exp(summed[-1])[:, None, None] * state + gained.reshape(heads, width, depth)
    return (advanced, result)

def run_blocks(inputs, log_decay, read_in, read_out, state):
    blocks = inputs.shape[0] // L
    pieces = (inputs.reshape(blocks, L, inputs.shape[1]), log_decay.reshape(blocks, L, log_decay.shape[1]), read_in.reshape(blocks, L, read_in.shape[1]), read_out.reshape(blocks, L, read_out.shape[1]))
    final, results = lax.scan(jax.checkpoint(block_advance), state, pieces)
    return (results.reshape(inputs.shape[0], inputs.shape[1]), final)

def reference(inputs, log_decay, read_in, read_out, initial_state, output_grad):
    (outputs, final), pullback = jax.vjp(run_blocks, inputs, log_decay, read_in, read_out, initial_state)
    grads = pullback((output_grad, jnp.zeros_like(final)))
    return (outputs, grads[0], grads[1], grads[2], grads[3], grads[4])
```

```python
import functools

import jax
import jax.numpy as jnp
from jax import lax
from jax.experimental import pallas as pl
from jax.experimental.pallas import tpu as pltpu
from jax.sharding import PartitionSpec as P

F32 = jnp.float32
BF16 = jnp.bfloat16
NN = ((1,), (0,))
NT = ((1,), (1,))
TN = ((0,), (0,))
MESH = pl.DeviceIdType.MESH


def dot(a, b, dims):
    return lax.dot_general(a, b, (dims, ((), ())), preferred_element_type=F32)


def exact_dot(a, b, dims):
    return lax.dot_general(
        a, b, (dims, ((), ())), preferred_element_type=F32, precision=lax.Precision.HIGHEST
    )


def split_dot(a, b, dims):
    high = a.astype(BF16)
    low = (a - high.astype(F32)).astype(BF16)
    return dot(high, b, dims) + dot(low, b, dims)


def iota(shape, axis):
    return lax.broadcasted_iota(jnp.int32, shape, axis)


def as_bf16(mask):
    return jnp.where(mask, 1.0, 0.0).astype(BF16)


def lower(length):
    return as_bf16(iota((length, length), 0) >= iota((length, length), 1))


def spread_sums(decay_ref, group, ratio, width):
    length, heads = decay_ref.shape
    columns = ratio * width
    pick = as_bf16(iota((heads, columns), 0) == group * ratio + iota((heads, columns), 1) // width)
    return dot(lower(length), dot(decay_ref[...], pick, NN).astype(BF16), NN)


def head_decays(decay_ref, group, ratio):
    length, heads = decay_ref.shape
    pick = as_bf16(iota((heads, ratio), 0) == group * ratio + iota((heads, ratio), 1))
    return dot(decay_ref[...], pick, NN).astype(BF16)


def gains_kernel(ratio, width, x_ref, decay_ref, in_ref, out_ref, grad_ref, gain_ref, own_ref, total_ref):
    group = pl.program_id(0)
    length = x_ref.shape[0]
    summed = spread_sums(decay_ref, group, ratio, width)
    weighted = (x_ref[...].astype(F32) * jnp.exp(summed[length - 1 :] - summed)).astype(BF16)
    gain_ref[...] = dot(weighted, in_ref[...], TN).astype(BF16)
    scaled = (grad_ref[...].astype(F32) * jnp.exp(summed)).astype(BF16)
    own_ref[...] = dot(scaled, out_ref[...], TN).astype(BF16)
    total_ref[...] = dot(head_decays(decay_ref, group, ratio), jnp.ones((length, 128), BF16), TN)


def gains(x, decay, read_in, read_out, grad, heads, width, depth):
    length = x.shape[0]
    groups = read_in.shape[1] // depth
    ratio = heads // groups
    columns = ratio * width
    wide = pl.BlockSpec((length, columns), lambda g: (0, g))
    narrow = pl.BlockSpec((length, depth), lambda g: (0, g))
    state = pl.BlockSpec((columns, depth), lambda g: (g, 0))
    return pl.pallas_call(
        functools.partial(gains_kernel, ratio, width),
        grid=(groups,),
        in_specs=[wide, pl.BlockSpec((length, heads), lambda g: (0, 0)), narrow, narrow, wide],
        out_specs=[state, state, pl.BlockSpec((ratio, 128), lambda g: (g, 0))],
        out_shape=[
            jax.ShapeDtypeStruct((heads * width, depth), BF16),
            jax.ShapeDtypeStruct((heads * width, depth), BF16),
            jax.ShapeDtypeStruct((heads, 128), F32),
        ],
        name="gains",
    )(x, decay, read_in, read_out, grad)


def carry_kernel(
    n_outer,
    n_inner,
    width,
    gain_ref,
    own_ref,
    total_ref,
    init_ref,
    state_ref,
    after_ref,
    start_ref,
    total1,
    gain1,
    own1,
    send_total,
    total2,
    send_gain,
    gain2,
    send_own,
    own2,
    send_before,
    before,
    send_behind,
    behind,
    send_state,
    send_after,
    inner_send,
    inner_recv,
    outer_send,
    outer_recv,
):
    outer = lax.axis_index("outer")
    inner = lax.axis_index("inner")
    heads = total1.shape[1]
    rows = gain2.shape[1]

    def inner_copy(stage, k, src, dst):
        to = lax.rem(inner + k, n_inner)
        return pltpu.make_async_remote_copy(
            src_ref=src.at[to],
            dst_ref=dst.at[inner],
            send_sem=inner_send.at[stage, k],
            recv_sem=inner_recv.at[stage, k],
            device_id=(outer, to),
            device_id_type=MESH,
        )

    def outer_copy(stage, k, src, dst):
        to = lax.rem(outer + k, n_outer)
        return pltpu.make_async_remote_copy(
            src_ref=src.at[to],
            dst_ref=dst.at[outer],
            send_sem=outer_send.at[stage, k],
            recv_sem=outer_recv.at[stage, k],
            device_id=(to, inner),
            device_id_type=MESH,
        )

    def each(n, act):
        def body(k, none):
            act(k)
            return none

        lax.fori_loop(1, n, body, 0)

    def start_inner(stage, src, dst):
        each(n_inner, lambda k: inner_copy(stage, k, src, dst).start())
        dst[inner] = src[inner]

    def recv_inner(stage, src, dst):
        each(n_inner, lambda k: inner_copy(stage, k, src, dst).wait_recv())

    def sent_inner(stage, src, dst):
        each(n_inner, lambda k: inner_copy(stage, k, src, dst).wait_send())

    def start_outer(stage, src, dst):
        each(n_outer, lambda k: outer_copy(stage, k, src, dst).start())
        dst[outer] = src[outer]

    def recv_outer(stage, src, dst):
        each(n_outer, lambda k: outer_copy(stage, k, src, dst).wait_recv())

    def sent_outer(stage, src, dst):
        each(n_outer, lambda k: outer_copy(stage, k, src, dst).wait_send())

    barrier = pltpu.get_barrier_semaphore()
    each(
        n_inner,
        lambda k: pl.semaphore_signal(
            barrier, inc=1, device_id=(outer, lax.rem(inner + k, n_inner)), device_id_type=MESH
        ),
    )
    each(
        n_outer,
        lambda k: pl.semaphore_signal(
            barrier, inc=1, device_id=(lax.rem(outer + k, n_outer), inner), device_id_type=MESH
        ),
    )
    pl.semaphore_wait(barrier, n_inner + n_outer - 2)

    start_inner(0, total_ref, total1)
    start_inner(1, gain_ref, gain1)
    recv_inner(0, total_ref, total1)

    def all_decay(k, none):
        head = k * rows // width
        row = total1[0, pl.ds(head, 1), :]
        for e in range(1, n_inner):
            row = row + total1[e, pl.ds(head, 1), :]
        send_total[k] = jnp.broadcast_to(row, send_total.shape[1:])
        return none

    lax.fori_loop(0, n_outer, all_decay, 0)
    start_outer(0, send_total, total2)

    sent_inner(1, gain_ref, gain1)
    start_inner(2, own_ref, own1)
    recv_inner(1, gain_ref, gain1)

    per_head = width // rows

    def factor(e, head):
        return jnp.exp(total1[e, pl.ds(head, 1), :])

    def group_gain(head, none):
        at = pl.ds(pl.multiple_of(head * width, width), width)
        value = gain1[0, at, :].astype(F32)
        for e in range(1, n_inner):
            value = factor(e, head) * value + gain1[e, at, :].astype(F32)
        value = value.astype(BF16)
        for i in range(per_head):
            send_gain[head * per_head + i] = value[i * rows : (i + 1) * rows]
        return none

    lax.fori_loop(0, heads, group_gain, 0)
    start_outer(1, send_gain, gain2)
    recv_outer(0, send_total, total2)
    recv_outer(1, send_gain, gain2)

    def scan_before(o, value):
        send_before[o] = value.astype(BF16)
        return jnp.exp(total2[o][0:1]) * value + gain2[o].astype(F32)

    lax.fori_loop(
        0, n_outer, scan_before, init_ref[pl.ds(pl.multiple_of(outer * rows, rows), rows), :]
    )
    start_outer(3, send_before, before)

    recv_inner(2, own_ref, own1)

    def group_own(head, none):
        at = pl.ds(pl.multiple_of(head * width, width), width)
        value = own1[n_inner - 1, at, :].astype(F32)
        for e in range(n_inner - 2, -1, -1):
            value = factor(e, head) * value + own1[e, at, :].astype(F32)
        value = value.astype(BF16)
        for i in range(per_head):
            send_own[head * per_head + i] = value[i * rows : (i + 1) * rows]
        return none

    lax.fori_loop(0, heads, group_own, 0)
    start_outer(2, send_own, own2)

    recv_outer(3, send_before, before)

    def block_states(head, none):
        at = pl.ds(pl.multiple_of(head * width, width), width)
        value = jnp.concatenate(
            [before[head * per_head + i].astype(F32) for i in range(per_head)], axis=0
        )
        for e in range(n_inner):
            send_state[e, at, :] = value.astype(BF16)
            if e < n_inner - 1:
                value = factor(e, head) * value + gain1[e, at, :].astype(F32)
        return none

    lax.fori_loop(0, heads, block_states, 0)
    start_inner(3, send_state, state_ref)

    recv_outer(2, send_own, own2)

    def scan_behind(i, value):
        o = n_outer - 1 - i
        send_behind[o, 0:rows, :] = value.astype(BF16)
        return jnp.exp(total2[o][0:1]) * value + own2[o].astype(F32)

    first = lax.fori_loop(0, n_outer, scan_behind, jnp.zeros(own2.shape[1:], F32)).astype(BF16)

    def add_first(o, none):
        send_behind[o, rows:, :] = first
        return none

    lax.fori_loop(0, n_outer, add_first, 0)
    start_outer(4, send_behind, behind)
    recv_outer(4, send_behind, behind)

    def block_after(head, none):
        at = pl.ds(pl.multiple_of(head * width, width), width)
        value = jnp.concatenate(
            [behind[head * per_head + i, 0:rows, :].astype(F32) for i in range(per_head)], axis=0
        )
        for e in range(n_inner - 1, -1, -1):
            send_after[e, at, :] = value.astype(BF16)
            if e > 0:
                value = factor(e, head) * value + own1[e, at, :].astype(F32)
        return none

    lax.fori_loop(0, heads, block_after, 0)
    start_inner(4, send_after, after_ref)

    def put_first(k, none):
        start_ref[k] = behind[k, rows:, :]
        return none

    lax.fori_loop(0, n_outer, put_first, 0)

    recv_inner(3, send_state, state_ref)
    recv_inner(4, send_after, after_ref)
    sent_inner(0, total_ref, total1)
    sent_inner(2, own_ref, own1)
    sent_inner(3, send_state, state_ref)
    sent_inner(4, send_after, after_ref)
    sent_outer(0, send_total, total2)
    sent_outer(1, send_gain, gain2)
    sent_outer(2, send_own, own2)
    sent_outer(3, send_before, before)
    sent_outer(4, send_behind, behind)


def carry(gain, own, total, init, n_outer, n_inner, width, depth):
    all_rows = gain.shape[0]
    chunk = all_rows // n_inner
    rows = chunk // n_outer
    heads = chunk // width
    vmem = pl.BlockSpec(memory_space=pltpu.VMEM)
    chunks = (n_inner, chunk, depth)
    pieces = (n_outer, rows, depth)
    doubles = (n_outer, 2 * rows, depth)
    totals = (n_outer, 8, depth)
    return pl.pallas_call(
        functools.partial(carry_kernel, n_outer, n_inner, width),
        in_specs=[vmem] * 4,
        out_specs=[vmem] * 3,
        out_shape=[
            jax.ShapeDtypeStruct(chunks, BF16),
            jax.ShapeDtypeStruct(chunks, BF16),
            jax.ShapeDtypeStruct(pieces, BF16),
        ],
        scratch_shapes=[
            pltpu.VMEM((n_inner, heads, depth), F32),
            pltpu.VMEM(chunks, BF16),
            pltpu.VMEM(chunks, BF16),
            pltpu.VMEM(totals, F32),
            pltpu.VMEM(totals, F32),
            pltpu.VMEM(pieces, BF16),
            pltpu.VMEM(pieces, BF16),
            pltpu.VMEM(pieces, BF16),
            pltpu.VMEM(pieces, BF16),
            pltpu.VMEM(pieces, BF16),
            pltpu.VMEM(pieces, BF16),
            pltpu.VMEM(doubles, BF16),
            pltpu.VMEM(doubles, BF16),
            pltpu.VMEM(chunks, BF16),
            pltpu.VMEM(chunks, BF16),
            pltpu.SemaphoreType.DMA((5, n_inner)),
            pltpu.SemaphoreType.DMA((5, n_inner)),
            pltpu.SemaphoreType.DMA((5, n_outer)),
            pltpu.SemaphoreType.DMA((5, n_outer)),
        ],
        compiler_params=pltpu.CompilerParams(
            collective_id=0, has_side_effects=True, vmem_limit_bytes=40 * 2**20
        ),
        name="carry",
    )(
        gain.reshape(chunks),
        own.reshape(chunks),
        total.reshape(n_inner, heads, depth),
        init,
    )


def block_kernel(
    ratio,
    width,
    x_ref,
    decay_ref,
    in_ref,
    out_ref,
    grad_ref,
    state_ref,
    after_ref,
    start_ref,
    y_ref,
    dx_ref,
    ddecay_ref,
    din_ref,
    dout_ref,
    dstart_ref,
    upper_sum,
    lower_sum,
    state_sum,
):
    group = pl.program_id(0)
    length = x_ref.shape[0]
    heads = decay_ref.shape[1]
    columns = ratio * width
    dstart_ref[...] = start_ref[...].astype(F32)

    summed = spread_sums(decay_ref, group, ratio, width)
    from_start = jnp.exp(summed)
    to_end = jnp.exp(summed[length - 1 :] - summed)
    picked = head_decays(decay_ref, group, ratio)
    low = lower(length)
    down = dot(low, picked, NN)
    across = dot(picked, low, ((0,), (1,)))
    x = x_ref[...]
    grad = grad_ref[...]
    x32 = x.astype(F32)
    grad32 = grad.astype(F32)
    b = in_ref[...]
    c = out_ref[...]
    state = state_ref[...]
    after = after_ref[...]
    scores = dot(c, b, NT)
    causal = iota((length, length), 0) >= iota((length, length), 1)

    local = []
    local_dx = []
    dscores = jnp.zeros((length, length), F32)
    for r in range(ratio):
        gap = down[:, r : r + 1] - across[r : r + 1, :]
        decays = jnp.exp(jnp.where(causal, gap, -1e30))
        weights = (scores * decays).astype(BF16)
        at = slice(r * width, (r + 1) * width)
        local.append(dot(weights, x[:, at], NN))
        local_dx.append(dot(weights, grad[:, at], TN))
        dscores = dscores + dot(grad[:, at], x[:, at], NT) * decays
    y = jnp.concatenate(local, axis=1) + dot(c, state, NT) * from_start
    y_ref[...] = y.astype(BF16)
    near_dx = jnp.concatenate(local_dx, axis=1)
    far_dx = dot(b, after, NT) * to_end
    dx_ref[...] = (near_dx + far_dx).astype(BF16)

    dscores = dscores.astype(BF16)
    dout_ref[...] = (
        dot(dscores, b, NN) + dot((grad32 * from_start).astype(BF16), state, NN)
    ).astype(BF16)
    din_ref[...] = (dot(dscores, c, TN) + dot((x32 * to_end).astype(BF16), after, NN)).astype(BF16)

    place = as_bf16(iota((columns, heads), 1) == group * ratio + iota((columns, heads), 0) // width)
    up = split_dot(y * grad32 - x32 * near_dx, place, NN)
    lo = split_dot(x32 * far_dx, place, NN)
    product = state.astype(F32) * after.astype(F32)
    total = dot(picked, jnp.ones((length, product.shape[1]), BF16), TN)
    state_sum[pl.ds(pl.multiple_of(group * ratio, ratio), ratio), :] = (
        jnp.sum(product.reshape(ratio, width, product.shape[1]), axis=1) * jnp.exp(total)
    )

    @pl.when(group == 0)
    def _():
        upper_sum[...] = up
        lower_sum[...] = lo

    @pl.when(group > 0)
    def _():
        upper_sum[...] += up
        lower_sum[...] += lo

    @pl.when(group == pl.num_programs(0) - 1)
    def _():
        row = iota((length, length), 0)
        column = iota((length, length), 1)
        up_mask = jnp.where(column >= row, 1.0, 0.0)
        low_mask = jnp.where(column < row, 1.0, 0.0)
        ones = jnp.ones((length, state_sum.shape[1]), F32)
        ddecay_ref[...] = (
            exact_dot(up_mask, upper_sum[...], NN)
            + exact_dot(low_mask, lower_sum[...], NN)
            + exact_dot(ones, state_sum[...], NT)
        ).astype(BF16)


def block(x, decay, read_in, read_out, grad, state, after, start, heads, width, depth):
    length = x.shape[0]
    groups = read_in.shape[1] // depth
    ratio = heads // groups
    columns = ratio * width
    share = start.shape[0] // groups
    wide = pl.BlockSpec((length, columns), lambda g: (0, g))
    narrow = pl.BlockSpec((length, depth), lambda g: (0, g))
    tall = pl.BlockSpec((columns, depth), lambda g: (g, 0))
    part = pl.BlockSpec((share, depth), lambda g: (g, 0))
    whole = pl.BlockSpec((length, heads), lambda g: (0, 0))
    return pl.pallas_call(
        functools.partial(block_kernel, ratio, width),
        grid=(groups,),
        in_specs=[wide, whole, narrow, narrow, wide, tall, tall, part],
        out_specs=[wide, wide, whole, narrow, narrow, part],
        out_shape=[
            jax.ShapeDtypeStruct(x.shape, BF16),
            jax.ShapeDtypeStruct(x.shape, BF16),
            jax.ShapeDtypeStruct(decay.shape, BF16),
            jax.ShapeDtypeStruct(read_in.shape, BF16),
            jax.ShapeDtypeStruct(read_out.shape, BF16),
            jax.ShapeDtypeStruct(start.shape, F32),
        ],
        scratch_shapes=[
            pltpu.VMEM((length, heads), F32),
            pltpu.VMEM((length, heads), F32),
            pltpu.VMEM((heads, depth), F32),
        ],
        name="block",
    )(x, decay, read_in, read_out, grad, state, after, start)


def shards(inputs, log_decay, read_in, read_out, initial_state, output_grad):
    n_outer, n_inner = lax.axis_size("outer"), lax.axis_size("inner")
    own_heads, width, depth = initial_state.shape
    heads = own_heads * n_inner
    gain, own, total = gains(
        inputs, log_decay, read_in, read_out, output_grad, heads, width, depth
    )
    state, after, start = carry(
        gain, own, total, initial_state.reshape(-1, depth), n_outer, n_inner, width, depth
    )
    y, dx, ddecay, din, dout, dstart = block(
        inputs,
        log_decay,
        read_in,
        read_out,
        output_grad,
        state.reshape(-1, depth),
        after.reshape(-1, depth),
        start.reshape(-1, depth),
        heads,
        width,
        depth,
    )
    return (y, dx, ddecay, din, dout, dstart.reshape(initial_state.shape))


def solution(mesh):
    tokens = P(("outer", "inner"), None)
    held = P("inner", None, None)
    return jax.shard_map(
        shards,
        mesh=mesh,
        in_specs=(tokens, tokens, tokens, tokens, held, tokens),
        out_specs=(tokens, tokens, tokens, tokens, tokens, held),
        check_vma=False,
    )
```

```python
import functools

import jax
import jax.numpy as jnp
from jax import lax
from jax.experimental import pallas as pl
from jax.experimental.pallas import tpu as pltpu
from jax.sharding import PartitionSpec as P

F32 = jnp.float32
BF16 = jnp.bfloat16
NN = ((1,), (0,))
NT = ((1,), (1,))
TN = ((0,), (0,))
MESH = pl.DeviceIdType.MESH


def dot(a, b, dims):
    return lax.dot_general(a, b, (dims, ((), ())), preferred_element_type=F32)


def exact_dot(a, b, dims):
    return lax.dot_general(
        a, b, (dims, ((), ())), preferred_element_type=F32, precision=lax.Precision.HIGHEST
    )


def split_dot(a, b, dims):
    high = a.astype(BF16)
    low = (a - high.astype(F32)).astype(BF16)
    return dot(high, b, dims) + dot(low, b, dims)


def iota(shape, axis):
    return lax.broadcasted_iota(jnp.int32, shape, axis)


def as_bf16(mask):
    return jnp.where(mask, 1.0, 0.0).astype(BF16)


def lower(length):
    return as_bf16(iota((length, length), 0) >= iota((length, length), 1))


def spread_sums(decay_ref, group, ratio, width):
    heads, length = decay_ref.shape
    columns = ratio * width
    pick = as_bf16(iota((heads, columns), 0) == group * ratio + iota((heads, columns), 1) // width)
    return dot(lower(length), dot(decay_ref[...], pick, TN).astype(BF16), NN)


def head_decays(decay_ref, group, ratio):
    heads, length = decay_ref.shape
    pick = as_bf16(iota((ratio, heads), 1) == group * ratio + iota((ratio, heads), 0))
    return dot(pick, decay_ref[...], NN).astype(BF16)


def carry_kernel(
    n_inner,
    n_low,
    n_high,
    ratio,
    width,
    x_hbm,
    decay_ref,
    in_hbm,
    out_hbm,
    grad_hbm,
    init_hbm,
    state_ref,
    after_ref,
    start_ref,
    x_ref,
    in_ref,
    out_ref,
    grad_ref,
    init_ref,
    send_total,
    total1,
    send_total2,
    total2,
    send_total3,
    total3,
    send_gain,
    gain1,
    send_own,
    own1,
    send_gain2,
    gain2,
    send_own2,
    own2,
    send_gain3,
    gain3,
    send_own3,
    own3,
    send_before,
    before,
    send_behind,
    behind,
    send_state,
    send_after,
    load_sem,
    inner_send,
    inner_recv,
    low_send,
    low_recv,
    high_send,
    high_recv,
):
    outer = lax.axis_index("outer")
    inner = lax.axis_index("inner")
    low = lax.rem(outer, n_low)
    high = lax.div(outer, n_low)
    length = x_ref.shape[0]
    depth = in_ref.shape[1] * ratio // decay_ref.shape[0]
    columns = ratio * width

    def inner_peer(k):
        return lax.rem(inner + k, n_inner)

    def low_peer(k):
        return lax.rem(low + k, n_low)

    def high_peer(k):
        return lax.rem(high + k, n_high)

    def inner_id(k):
        return (outer, inner_peer(k))

    def low_id(k):
        return (high * n_low + low_peer(k), inner)

    def high_id(k):
        return (high_peer(k) * n_low + low, inner)

    def each(n, act):
        def body(k, none):
            act(k)
            return none

        lax.fori_loop(1, n, body, 0)

    def remote(src, dst, send, recv, to):
        return pltpu.make_async_remote_copy(
            src_ref=src,
            dst_ref=dst,
            send_sem=send,
            recv_sem=recv,
            device_id=to,
            device_id_type=MESH,
        )

    def inner_copy(stage, k, src, dst, at=slice(None)):
        return remote(
            src.at[inner_peer(k), at],
            dst.at[inner, at],
            inner_send.at[stage, k],
            inner_recv.at[stage, k],
            inner_id(k),
        )

    def low_copy(stage, k, src, dst, half):
        return remote(
            src.at[half, low_peer(k)],
            dst.at[half, low],
            low_send.at[stage, k],
            low_recv.at[stage, k],
            low_id(k),
        )

    def high_copy(stage, k, src, dst, half):
        return remote(
            src.at[half],
            dst.at[half, high],
            high_send.at[stage, k],
            high_recv.at[stage, k],
            high_id(k),
        )

    def total_copy(k):
        return remote(
            send_total.at[inner_peer(k)],
            total1.at[inner],
            inner_send.at[0, k],
            inner_recv.at[0, k],
            inner_id(k),
        )

    def total2_copy(k):
        return remote(
            send_total2, total2.at[low], low_send.at[0, k], low_recv.at[0, k], low_id(k)
        )

    def total3_copy(k):
        return remote(
            send_total3, total3.at[high], high_send.at[0, k], high_recv.at[0, k], high_id(k)
        )

    loads = [
        pltpu.make_async_copy(src, dst, load_sem.at[i])
        for i, (src, dst) in enumerate(
            ((x_hbm, x_ref), (in_hbm, in_ref), (grad_hbm, grad_ref), (out_hbm, out_ref))
        )
    ]
    for half in range(2):
        rows = pl.ds(pl.multiple_of((half * ratio + low) * width, width), width)
        loads.append(
            pltpu.make_async_copy(init_hbm.at[rows], init_ref.at[half], load_sem.at[4 + half])
        )
    for load in loads:
        load.start()

    barrier = pltpu.get_barrier_semaphore()
    for n, peer in ((n_inner, inner_id), (n_low, low_id), (n_high, high_id)):
        each(
            n,
            lambda k, peer=peer: pl.semaphore_signal(
                barrier, inc=1, device_id=peer(k), device_id_type=MESH
            ),
        )

    totals = dot(decay_ref[...], jnp.ones((length, send_total.shape[2]), BF16), NN)
    for e in range(n_inner):
        send_total[e] = totals[e * 2 * ratio : (e + 1) * 2 * ratio]

    pl.semaphore_wait(barrier, n_inner + n_low + n_high - 3)
    each(n_inner, lambda k: total_copy(k).start())
    total1[inner] = send_total[inner]

    def half_rows(half):
        return pl.ds(half * columns, columns)

    def group_slices(group):
        return (
            pl.ds(pl.multiple_of(group * columns, columns), columns),
            pl.ds(pl.multiple_of(group * depth, depth), depth),
        )

    def gain_of(half, k):
        to = inner_peer(k)
        wide, narrow = group_slices(2 * to + half)
        summed = spread_sums(decay_ref, 2 * to + half, ratio, width)
        weighted = x_ref[:, wide].astype(F32) * jnp.exp(summed[length - 1 :] - summed)
        return dot(weighted.astype(BF16), in_ref[:, narrow], TN).astype(BF16)

    def own_of(half, k):
        to = inner_peer(k)
        wide, narrow = group_slices(2 * to + half)
        summed = spread_sums(decay_ref, 2 * to + half, ratio, width)
        scaled = grad_ref[:, wide].astype(F32) * jnp.exp(summed)
        return dot(scaled.astype(BF16), out_ref[:, narrow], TN).astype(BF16)

    def send_gains(half):
        at = half_rows(half)

        def act(k):
            send_gain[inner_peer(k), at, :] = gain_of(half, k)
            inner_copy(1 + half, k, send_gain, gain1, at).start()

        each(n_inner, act)
        gain1[inner, at, :] = gain_of(half, 0)

    def fill_owns(half):
        at = half_rows(half)

        def act(k):
            send_own[inner_peer(k), at, :] = own_of(half, k)

        each(n_inner, act)
        own1[inner, at, :] = own_of(half, 0)

    def send_inner(stage, src, dst, half):
        each(n_inner, lambda k: inner_copy(stage + half, k, src, dst, half_rows(half)).start())

    def recv_inner(stage, src, dst, half):
        each(n_inner, lambda k: inner_copy(stage + half, k, src, dst, half_rows(half)).wait_recv())

    def sent_inner(stage, src, dst, half):
        each(n_inner, lambda k: inner_copy(stage + half, k, src, dst, half_rows(half)).wait_send())

    def keep_inner(src, dst, half):
        at = half_rows(half)
        dst[inner, at, :] = src[inner, at, :]

    def send_low(stage, src, dst, half):
        each(n_low, lambda k: low_copy(stage + half, k, src, dst, half).start())
        dst[half, low] = src[half, low]

    def recv_low(stage, src, dst, half):
        each(n_low, lambda k: low_copy(stage + half, k, src, dst, half).wait_recv())

    def sent_low(stage, src, dst, half):
        each(n_low, lambda k: low_copy(stage + half, k, src, dst, half).wait_send())

    def send_high(stage, src, dst, half):
        each(n_high, lambda k: high_copy(stage + half, k, src, dst, half).start())
        dst[half, high] = src[half]

    def recv_high(stage, src, dst, half):
        each(n_high, lambda k: high_copy(stage + half, k, src, dst, half).wait_recv())

    def sent_high(stage, src, dst, half):
        each(n_high, lambda k: high_copy(stage + half, k, src, dst, half).wait_send())

    def factor1(e, head):
        return jnp.exp(total1[e, pl.ds(head, 1), :])

    def factor2(e, half):
        return jnp.exp(total2[e, pl.ds(half * ratio + low, 1), :])

    def factor3(e, half):
        return jnp.exp(total3[e, pl.ds(half * ratio + low, 1), :])

    def head_rows(head):
        return pl.ds(pl.multiple_of(head * width, width), width)

    def fold_gains(half):
        def body(r, none):
            head = half * ratio + r
            at = head_rows(head)
            value = gain1[0, at, :].astype(F32)
            for e in range(1, n_inner):
                value = factor1(e, head) * value + gain1[e, at, :].astype(F32)
            send_gain2[half, r] = value.astype(BF16)
            return none

        lax.fori_loop(0, ratio, body, 0)

    def fold_owns(half):
        def body(r, none):
            head = half * ratio + r
            at = head_rows(head)
            value = own1[n_inner - 1, at, :].astype(F32)
            for e in range(n_inner - 2, -1, -1):
                value = factor1(e, head) * value + own1[e, at, :].astype(F32)
            send_own2[half, r] = value.astype(BF16)
            return none

        lax.fori_loop(0, ratio, body, 0)

    def fold_gains2(half):
        value = gain2[half, 0].astype(F32)
        for e in range(1, n_low):
            value = factor2(e, half) * value + gain2[half, e].astype(F32)
        send_gain3[half] = value.astype(BF16)

    def fold_owns2(half):
        value = own2[half, n_low - 1].astype(F32)
        for e in range(n_low - 2, -1, -1):
            value = factor2(e, half) * value + own2[half, e].astype(F32)
        send_own3[half] = value.astype(BF16)

    def spread_states(half):
        value = init_ref[half]
        for e in range(n_high - 1):
            later = factor3(e, half) * value + gain3[half, e].astype(F32)
            value = jnp.where(e < high, later, value)
        for e in range(n_low):
            send_before[half, e] = value.astype(BF16)
            if e < n_low - 1:
                value = factor2(e, half) * value + gain2[half, e].astype(F32)

    def spread_afters(half):
        value = jnp.zeros(init_ref.shape[1:], F32)
        first = value
        for e in range(n_high - 1, -1, -1):
            first = factor3(e, half) * first + own3[half, e].astype(F32)
            value = jnp.where(e > high, first, value)
        first = first.astype(BF16)
        for e in range(n_low - 1, -1, -1):
            send_behind[half, e, 0:width] = value.astype(BF16)
            send_behind[half, e, width:] = first
            if e > 0:
                value = factor2(e, half) * value + own2[half, e].astype(F32)

    def fill_states(half):
        def body(r, none):
            head = half * ratio + r
            at = head_rows(head)
            value = before[half, r].astype(F32)
            for e in range(n_inner):
                send_state[e, at, :] = value.astype(BF16)
                if e < n_inner - 1:
                    value = factor1(e, head) * value + gain1[e, at, :].astype(F32)
            return none

        lax.fori_loop(0, ratio, body, 0)
        keep_inner(send_state, state_ref, half)

    def fill_afters(half):
        def body(r, none):
            head = half * ratio + r
            at = head_rows(head)
            start_ref[at, :] = behind[half, r, width:]
            value = behind[half, r, 0:width].astype(F32)
            for e in range(n_inner - 1, -1, -1):
                send_after[e, at, :] = value.astype(BF16)
                if e > 0:
                    value = factor1(e, head) * value + own1[e, at, :].astype(F32)
            return none

        lax.fori_loop(0, ratio, body, 0)
        keep_inner(send_after, after_ref, half)

    gains, owns = (1, send_gain, gain1), (3, send_own, own1)
    states, afters = (5, send_state, state_ref), (7, send_after, after_ref)
    gains2, owns2 = (1, send_gain2, gain2), (3, send_own2, own2)
    befores, behinds = (5, send_before, before), (7, send_behind, behind)
    gains3, owns3 = (1, send_gain3, gain3), (3, send_own3, own3)

    loads[0].wait()
    loads[1].wait()
    send_gains(0)
    send_gains(1)

    each(n_inner, lambda k: total_copy(k).wait_recv())
    row = total1[0]
    for e in range(1, n_inner):
        row = row + total1[e]
    send_total2[...] = row
    each(n_low, lambda k: total2_copy(k).start())
    total2[low] = row

    loads[2].wait()
    loads[3].wait()
    fill_owns(0)
    fill_owns(1)

    each(n_low, lambda k: total2_copy(k).wait_recv())
    row = total2[0]
    for e in range(1, n_low):
        row = row + total2[e]
    send_total3[...] = row
    each(n_high, lambda k: total3_copy(k).start())
    total3[high] = row

    recv_inner(*gains, 0)
    fold_gains(0)
    send_low(*gains2, 0)
    sent_inner(*gains, 0)
    sent_inner(*gains, 1)
    send_inner(*owns, 0)
    recv_low(*gains2, 0)
    fold_gains2(0)
    send_high(*gains3, 0)
    each(n_high, lambda k: total3_copy(k).wait_recv())
    loads[4].wait()
    loads[5].wait()
    recv_inner(*gains, 1)
    fold_gains(1)
    send_low(*gains2, 1)
    recv_high(*gains3, 0)
    spread_states(0)
    send_low(*befores, 0)
    recv_low(*gains2, 1)
    fold_gains2(1)
    send_high(*gains3, 1)
    sent_inner(*owns, 0)
    send_inner(*owns, 1)
    recv_high(*gains3, 1)
    spread_states(1)
    send_low(*befores, 1)
    recv_inner(*owns, 0)
    fold_owns(0)
    send_low(*owns2, 0)
    recv_low(*befores, 0)
    fill_states(0)
    recv_low(*owns2, 0)
    fold_owns2(0)
    send_high(*owns3, 0)
    recv_low(*befores, 1)
    fill_states(1)
    sent_inner(*owns, 1)
    send_inner(*states, 0)
    recv_inner(*owns, 1)
    fold_owns(1)
    send_low(*owns2, 1)
    recv_high(*owns3, 0)
    spread_afters(0)
    send_low(*behinds, 0)
    recv_low(*owns2, 1)
    fold_owns2(1)
    send_high(*owns3, 1)
    sent_inner(*states, 0)
    send_inner(*states, 1)
    recv_high(*owns3, 1)
    spread_afters(1)
    send_low(*behinds, 1)
    recv_low(*behinds, 0)
    fill_afters(0)
    sent_inner(*states, 1)
    send_inner(*afters, 0)
    recv_low(*behinds, 1)
    fill_afters(1)
    sent_inner(*afters, 0)
    send_inner(*afters, 1)

    each(n_inner, lambda k: total_copy(k).wait_send())
    each(n_low, lambda k: total2_copy(k).wait_send())
    each(n_high, lambda k: total3_copy(k).wait_send())
    for half in range(2):
        for stage in (gains2, owns2, befores, behinds):
            sent_low(*stage, half)
        for stage in (gains3, owns3):
            sent_high(*stage, half)
        recv_inner(*states, half)
    recv_inner(*afters, 0)
    recv_inner(*afters, 1)
    sent_inner(*afters, 1)


def carry(x, decay, read_in, read_out, grad, init, n_outer, n_inner, width, depth):
    length = x.shape[0]
    groups = read_in.shape[1] // depth
    heads = decay.shape[0]
    ratio = heads // groups
    mine = heads // n_inner
    n_low = ratio
    n_high = n_outer // n_low
    vmem = pl.BlockSpec(memory_space=pltpu.VMEM)
    hbm = pl.BlockSpec(memory_space=pl.ANY)
    chunks = pltpu.VMEM((n_inner, mine * width, depth), BF16)
    runs = pltpu.VMEM((2, n_low, width, depth), BF16)
    doubles = pltpu.VMEM((2, n_low, 2 * width, depth), BF16)
    head = pltpu.VMEM((2, width, depth), BF16)
    highs = pltpu.VMEM((2, n_high, width, depth), BF16)
    total = pltpu.VMEM((mine, depth), F32)
    state = jax.ShapeDtypeStruct((n_inner, mine * width, depth), BF16)
    dma = pltpu.SemaphoreType.DMA
    return pl.pallas_call(
        functools.partial(carry_kernel, n_inner, n_low, n_high, ratio, width),
        in_specs=[hbm, vmem, hbm, hbm, hbm, hbm],
        out_specs=[vmem] * 3,
        out_shape=[state, state, jax.ShapeDtypeStruct((mine * width, depth), BF16)],
        scratch_shapes=[
            pltpu.VMEM(x.shape, BF16),
            pltpu.VMEM(read_in.shape, BF16),
            pltpu.VMEM(read_out.shape, BF16),
            pltpu.VMEM(grad.shape, BF16),
            pltpu.VMEM((2, width, depth), F32),
            pltpu.VMEM((n_inner, mine, depth), F32),
            pltpu.VMEM((n_inner, mine, depth), F32),
            total,
            pltpu.VMEM((n_low, mine, depth), F32),
            total,
            pltpu.VMEM((n_high, mine, depth), F32),
            chunks,
            chunks,
            chunks,
            chunks,
            runs,
            runs,
            runs,
            runs,
            head,
            highs,
            head,
            highs,
            runs,
            runs,
            doubles,
            doubles,
            chunks,
            chunks,
            dma((6,)),
            dma((9, n_inner)),
            dma((9, n_inner)),
            dma((9, n_low)),
            dma((9, n_low)),
            dma((5, n_high)),
            dma((5, n_high)),
        ],
        compiler_params=pltpu.CompilerParams(
            collective_id=0, has_side_effects=True, vmem_limit_bytes=48 * 2**20
        ),
        name="carry",
    )(x, decay, read_in, read_out, grad, init)


def block_kernel(
    ratio,
    width,
    x_ref,
    decay_ref,
    in_ref,
    out_ref,
    grad_ref,
    state_ref,
    after_ref,
    start_ref,
    y_ref,
    dx_ref,
    ddecay_ref,
    din_ref,
    dout_ref,
    dstart_ref,
    upper_sum,
    lower_sum,
    state_sum,
):
    group = pl.program_id(0)
    length = x_ref.shape[0]
    heads = decay_ref.shape[0]
    columns = ratio * width
    dstart_ref[...] = start_ref[...].astype(F32)

    summed = spread_sums(decay_ref, group, ratio, width)
    from_start = jnp.exp(summed)
    to_end = jnp.exp(summed[length - 1 :] - summed)
    picked = head_decays(decay_ref, group, ratio)
    low = lower(length)
    down = dot(low, picked, NT)
    across = dot(picked, low, NT)
    x = x_ref[...]
    grad = grad_ref[...]
    x32 = x.astype(F32)
    grad32 = grad.astype(F32)
    b = in_ref[...]
    c = out_ref[...]
    state = state_ref[...]
    after = after_ref[...]
    scores = dot(c, b, NT)
    causal = iota((length, length), 0) >= iota((length, length), 1)

    local = []
    local_dx = []
    dscores = jnp.zeros((length, length), F32)
    for r in range(ratio):
        gap = down[:, r : r + 1] - across[r : r + 1, :]
        decays = jnp.exp(jnp.where(causal, gap, -1e30))
        weights = (scores * decays).astype(BF16)
        at = slice(r * width, (r + 1) * width)
        local.append(dot(weights, x[:, at], NN))
        local_dx.append(dot(weights, grad[:, at], TN))
        dscores = dscores + dot(grad[:, at], x[:, at], NT) * decays
    y = jnp.concatenate(local, axis=1) + dot(c, state, NT) * from_start
    y_ref[...] = y.astype(BF16)
    near_dx = jnp.concatenate(local_dx, axis=1)
    far_dx = dot(b, after, NT) * to_end
    dx_ref[...] = (near_dx + far_dx).astype(BF16)

    dscores = dscores.astype(BF16)
    dout_ref[...] = (
        dot(dscores, b, NN) + dot((grad32 * from_start).astype(BF16), state, NN)
    ).astype(BF16)
    din_ref[...] = (dot(dscores, c, TN) + dot((x32 * to_end).astype(BF16), after, NN)).astype(BF16)

    place = as_bf16(iota((columns, heads), 1) == group * ratio + iota((columns, heads), 0) // width)
    up = split_dot(y * grad32 - x32 * near_dx, place, NN)
    lo = split_dot(x32 * far_dx, place, NN)
    product = state.astype(F32) * after.astype(F32)
    total = dot(picked, jnp.ones((length, product.shape[1]), BF16), NN)
    state_sum[pl.ds(pl.multiple_of(group * ratio, ratio), ratio), :] = (
        jnp.sum(product.reshape(ratio, width, product.shape[1]), axis=1) * jnp.exp(total)
    )

    @pl.when(group == 0)
    def _():
        upper_sum[...] = up
        lower_sum[...] = lo

    @pl.when(group > 0)
    def _():
        upper_sum[...] += up
        lower_sum[...] += lo

    @pl.when(group == pl.num_programs(0) - 1)
    def _():
        row = iota((length, length), 0)
        column = iota((length, length), 1)
        up_mask = jnp.where(row >= column, 1.0, 0.0)
        low_mask = jnp.where(row < column, 1.0, 0.0)
        ddecay_ref[...] = (
            exact_dot(upper_sum[...], up_mask, TN)
            + exact_dot(lower_sum[...], low_mask, TN)
            + jnp.sum(state_sum[...], axis=1, keepdims=True)
        ).astype(BF16)


def block(x, decay, read_in, read_out, grad, state, after, start, heads, width, depth):
    length = x.shape[0]
    groups = read_in.shape[1] // depth
    ratio = heads // groups
    columns = ratio * width
    share = start.shape[0] // groups
    wide = pl.BlockSpec((length, columns), lambda g: (0, g))
    narrow = pl.BlockSpec((length, depth), lambda g: (0, g))
    tall = pl.BlockSpec((columns, depth), lambda g: (g, 0))
    part = pl.BlockSpec((share, depth), lambda g: (g, 0))
    whole = pl.BlockSpec((heads, length), lambda g: (0, 0))
    return pl.pallas_call(
        functools.partial(block_kernel, ratio, width),
        grid=(groups,),
        in_specs=[wide, whole, narrow, narrow, wide, tall, tall, part],
        out_specs=[wide, wide, whole, narrow, narrow, part],
        out_shape=[
            jax.ShapeDtypeStruct(x.shape, BF16),
            jax.ShapeDtypeStruct(x.shape, BF16),
            jax.ShapeDtypeStruct(decay.shape, BF16),
            jax.ShapeDtypeStruct(read_in.shape, BF16),
            jax.ShapeDtypeStruct(read_out.shape, BF16),
            jax.ShapeDtypeStruct(start.shape, F32),
        ],
        scratch_shapes=[
            pltpu.VMEM((length, heads), F32),
            pltpu.VMEM((length, heads), F32),
            pltpu.VMEM((heads, depth), F32),
        ],
        name="block",
    )(x, decay, read_in, read_out, grad, state, after, start)


def shards(inputs, log_decay, read_in, read_out, initial_state, output_grad):
    n_outer, n_inner = lax.axis_size("outer"), lax.axis_size("inner")
    own_heads, width, depth = initial_state.shape
    heads = own_heads * n_inner
    decay = log_decay.T
    tokens = (inputs, decay, read_in, read_out, output_grad)
    state, after, start = carry(
        *tokens, initial_state.reshape(-1, depth), n_outer, n_inner, width, depth
    )
    y, dx, ddecay, din, dout, dstart = block(
        *tokens,
        state.reshape(-1, depth),
        after.reshape(-1, depth),
        start,
        heads,
        width,
        depth,
    )
    return (y, dx, ddecay.T, din, dout, dstart.reshape(initial_state.shape))


def solution(mesh):
    tokens = P(("outer", "inner"), None)
    held = P("inner", None, None)
    return jax.shard_map(
        shards,
        mesh=mesh,
        in_specs=(tokens, tokens, tokens, tokens, held, tokens),
        out_specs=(tokens, tokens, tokens, tokens, tokens, held),
        check_vma=False,
    )
```

```python
import functools

import jax
import jax.numpy as jnp
from jax import lax
from jax.experimental import pallas as pl
from jax.experimental.pallas import tpu as pltpu
from jax.sharding import PartitionSpec as P

F32 = jnp.float32
BF16 = jnp.bfloat16
NN = ((1,), (0,))
NT = ((1,), (1,))
TN = ((0,), (0,))
MESH = pl.DeviceIdType.MESH


def dot(a, b, dims):
    return lax.dot_general(a, b, (dims, ((), ())), preferred_element_type=F32)


def exact_dot(a, b, dims):
    return lax.dot_general(
        a, b, (dims, ((), ())), preferred_element_type=F32, precision=lax.Precision.HIGHEST
    )


def split_dot(a, b, dims):
    high = a.astype(BF16)
    low = (a - high.astype(F32)).astype(BF16)
    return dot(high, b, dims) + dot(low, b, dims)


def iota(shape, axis):
    return lax.broadcasted_iota(jnp.int32, shape, axis)


def as_bf16(mask):
    return jnp.where(mask, 1.0, 0.0).astype(BF16)


def lower(length):
    return as_bf16(iota((length, length), 0) >= iota((length, length), 1))


def spread_sums(decay_ref, group, ratio, width):
    heads, length = decay_ref.shape
    columns = ratio * width
    pick = as_bf16(iota((heads, columns), 0) == group * ratio + iota((heads, columns), 1) // width)
    return dot(lower(length), dot(decay_ref[...], pick, TN).astype(BF16), NN)


def head_decays(decay_ref, group, ratio):
    heads, length = decay_ref.shape
    pick = as_bf16(iota((ratio, heads), 1) == group * ratio + iota((ratio, heads), 0))
    return dot(pick, decay_ref[...], NN).astype(BF16)


def carry_kernel(
    n_inner,
    n_low,
    n_high,
    ratio,
    width,
    x_hbm,
    decay_ref,
    in_hbm,
    out_hbm,
    grad_hbm,
    init_hbm,
    y_hbm,
    dx_hbm,
    ddecay_hbm,
    din_hbm,
    dout_hbm,
    dstart_hbm,
    state_ref,
    after_ref,
    start_ref,
    from_start,
    to_end,
    weighted_ref,
    scaled_ref,
    y_sum,
    dx_sum,
    din_sum,
    dout_sum,
    up_sum,
    low_sum,
    state_sum,
    y_ref,
    dx_ref,
    ddecay_ref,
    din_ref,
    dout_ref,
    x_ref,
    in_ref,
    out_ref,
    grad_ref,
    init_ref,
    send_total,
    total1,
    send_total2,
    total2,
    send_total3,
    total3,
    send_gain,
    gain1,
    send_own,
    own1,
    send_gain2,
    gain2,
    send_own2,
    own2,
    send_gain3,
    gain3,
    send_own3,
    own3,
    send_before,
    before,
    send_behind,
    behind,
    send_state,
    send_after,
    load_sem,
    store_sem,
    inner_send,
    inner_recv,
    low_send,
    low_recv,
    high_send,
    high_recv,
):
    outer = lax.axis_index("outer")
    inner = lax.axis_index("inner")
    low = lax.rem(outer, n_low)
    high = lax.div(outer, n_low)
    length = x_ref.shape[0]
    depth = in_ref.shape[1] * ratio // decay_ref.shape[0]
    columns = ratio * width

    def inner_peer(k):
        return lax.rem(inner + k, n_inner)

    def low_peer(k):
        return lax.rem(low + k, n_low)

    def high_peer(k):
        return lax.rem(high + k, n_high)

    def inner_id(k):
        return (outer, inner_peer(k))

    def low_id(k):
        return (high * n_low + low_peer(k), inner)

    def high_id(k):
        return (high_peer(k) * n_low + low, inner)

    def each(n, act):
        def body(k, none):
            act(k)
            return none

        lax.fori_loop(1, n, body, 0)

    def remote(src, dst, send, recv, to):
        return pltpu.make_async_remote_copy(
            src_ref=src,
            dst_ref=dst,
            send_sem=send,
            recv_sem=recv,
            device_id=to,
            device_id_type=MESH,
        )

    def inner_copy(stage, k, src, dst, at=slice(None)):
        return remote(
            src.at[inner_peer(k), at],
            dst.at[inner, at],
            inner_send.at[stage, k],
            inner_recv.at[stage, k],
            inner_id(k),
        )

    def low_copy(stage, k, src, dst, half):
        return remote(
            src.at[half, low_peer(k)],
            dst.at[half, low],
            low_send.at[stage, k],
            low_recv.at[stage, k],
            low_id(k),
        )

    def high_copy(stage, k, src, dst, half):
        return remote(
            src.at[half],
            dst.at[half, high],
            high_send.at[stage, k],
            high_recv.at[stage, k],
            high_id(k),
        )

    def total_copy(k):
        return remote(
            send_total.at[inner_peer(k)],
            total1.at[inner],
            inner_send.at[0, k],
            inner_recv.at[0, k],
            inner_id(k),
        )

    def total2_copy(k):
        return remote(
            send_total2, total2.at[low], low_send.at[0, k], low_recv.at[0, k], low_id(k)
        )

    def total3_copy(k):
        return remote(
            send_total3, total3.at[high], high_send.at[0, k], high_recv.at[0, k], high_id(k)
        )

    loads = [
        pltpu.make_async_copy(src, dst, load_sem.at[i])
        for i, (src, dst) in enumerate(
            ((x_hbm, x_ref), (in_hbm, in_ref), (grad_hbm, grad_ref), (out_hbm, out_ref))
        )
    ]
    for half in range(2):
        rows = pl.ds(pl.multiple_of((half * ratio + low) * width, width), width)
        loads.append(
            pltpu.make_async_copy(init_hbm.at[rows], init_ref.at[half], load_sem.at[4 + half])
        )
    for load in loads:
        load.start()

    barrier = pltpu.get_barrier_semaphore()
    for n, peer in ((n_inner, inner_id), (n_low, low_id), (n_high, high_id)):
        each(
            n,
            lambda k, peer=peer: pl.semaphore_signal(
                barrier, inc=1, device_id=peer(k), device_id_type=MESH
            ),
        )

    totals = dot(decay_ref[...], jnp.ones((length, send_total.shape[2]), BF16), NN)
    for e in range(n_inner):
        send_total[e] = totals[e * 2 * ratio : (e + 1) * 2 * ratio]

    pl.semaphore_wait(barrier, n_inner + n_low + n_high - 3)
    each(n_inner, lambda k: total_copy(k).start())
    total1[inner] = send_total[inner]

    def half_rows(half):
        return pl.ds(half * columns, columns)

    def group_slices(group):
        return (
            pl.ds(pl.multiple_of(group * columns, columns), columns),
            pl.ds(pl.multiple_of(group * depth, depth), depth),
        )

    def gain_of(half, k):
        group = 2 * inner_peer(k) + half
        wide, narrow = group_slices(group)
        summed = spread_sums(decay_ref, group, ratio, width)
        from_start[:, wide] = jnp.exp(summed)
        factor = jnp.exp(summed[length - 1 :] - summed)
        to_end[:, wide] = factor
        weighted = (x_ref[:, wide].astype(F32) * factor).astype(BF16)
        weighted_ref[:, wide] = weighted
        return dot(weighted, in_ref[:, narrow], TN).astype(BF16)

    def own_of(half, k):
        wide, narrow = group_slices(2 * inner_peer(k) + half)
        scaled = (grad_ref[:, wide].astype(F32) * from_start[:, wide]).astype(BF16)
        scaled_ref[:, wide] = scaled
        return dot(scaled, out_ref[:, narrow], TN).astype(BF16)

    def local_part(group):
        wide, narrow = group_slices(group)
        picked = head_decays(decay_ref, group, ratio)
        below = lower(length)
        down = dot(below, picked, NT)
        across = dot(picked, below, NT)
        x, grad = x_ref[:, wide], grad_ref[:, wide]
        b, c = in_ref[:, narrow], out_ref[:, narrow]
        scores = dot(c, b, NT)
        causal = iota((length, length), 0) >= iota((length, length), 1)
        ys, dxs = [], []
        dscores = jnp.zeros((length, length), F32)
        for r in range(ratio):
            gap = down[:, r : r + 1] - across[r : r + 1, :]
            decays = jnp.exp(jnp.where(causal, gap, -1e30))
            weights = (scores * decays).astype(BF16)
            at = slice(r * width, (r + 1) * width)
            ys.append(dot(weights, x[:, at], NN))
            dxs.append(dot(weights, grad[:, at], TN))
            dscores = dscores + dot(grad[:, at], x[:, at], NT) * decays
        y_sum[:, wide] = jnp.concatenate(ys, axis=1)
        dx_sum[:, wide] = jnp.concatenate(dxs, axis=1)
        dscores = dscores.astype(BF16)
        dout_sum[:, narrow] = dot(dscores, b, NN)
        din_sum[:, narrow] = dot(dscores, c, TN)

    def place(group):
        heads = decay_ref.shape[0]
        head = group * ratio + iota((columns, heads), 0) // width
        return as_bf16(iota((columns, heads), 1) == head)

    def state_part(half, k):
        owner = inner_peer(n_inner - k)
        group = 2 * owner + half
        wide, narrow = group_slices(group)
        state = state_ref[owner, half_rows(half), :]
        y = y_sum[:, wide] + dot(out_ref[:, narrow], state, NT) * from_start[:, wide]
        y_ref[:, wide] = y.astype(BF16)
        dout = dout_sum[:, narrow] + dot(scaled_ref[:, wide], state, NN)
        dout_ref[:, narrow] = dout.astype(BF16)
        change = y * grad_ref[:, wide].astype(F32) - x_ref[:, wide].astype(F32) * dx_sum[:, wide]
        up_sum[...] += split_dot(change, place(group), NN)

    def after_part(half, k):
        owner = inner_peer(n_inner - k)
        group = 2 * owner + half
        wide, narrow = group_slices(group)
        state = state_ref[owner, half_rows(half), :]
        after = after_ref[owner, half_rows(half), :]
        far = dot(in_ref[:, narrow], after, NT) * to_end[:, wide]
        dx_ref[:, wide] = (dx_sum[:, wide] + far).astype(BF16)
        din = din_sum[:, narrow] + dot(weighted_ref[:, wide], after, NN)
        din_ref[:, narrow] = din.astype(BF16)
        low_sum[...] += split_dot(x_ref[:, wide].astype(F32) * far, place(group), NN)
        product = state.astype(F32) * after.astype(F32)
        picked = head_decays(decay_ref, group, ratio)
        total = dot(picked, jnp.ones((length, depth), BF16), NN)
        state_sum[pl.ds(pl.multiple_of(group * ratio, ratio), ratio), :] = jnp.sum(
            product.reshape(ratio, width, depth), axis=1
        ) * jnp.exp(total)

    def local_parts(start, stop):
        def body(group, none):
            local_part(group)
            return none

        groups = n_inner * 2
        lax.fori_loop(start * groups // 8, stop * groups // 8, body, 0)

    def parts(stage, half, part):
        part(half, 0)

        def act(k):
            inner_copy(stage[0] + half, k, stage[1], stage[2], half_rows(half)).wait_recv()
            part(half, k)

        each(n_inner, act)

    def store(i, src, dst):
        return pltpu.make_async_copy(src, dst, store_sem.at[i])

    def send_gains(half):
        at = half_rows(half)

        def act(k):
            send_gain[inner_peer(k), at, :] = gain_of(half, k)
            inner_copy(1 + half, k, send_gain, gain1, at).start()

        each(n_inner, act)
        gain1[inner, at, :] = gain_of(half, 0)

    def fill_owns(half):
        at = half_rows(half)

        def act(k):
            send_own[inner_peer(k), at, :] = own_of(half, k)

        each(n_inner, act)
        own1[inner, at, :] = own_of(half, 0)

    def send_inner(stage, src, dst, half):
        each(n_inner, lambda k: inner_copy(stage + half, k, src, dst, half_rows(half)).start())

    def recv_inner(stage, src, dst, half):
        each(n_inner, lambda k: inner_copy(stage + half, k, src, dst, half_rows(half)).wait_recv())

    def sent_inner(stage, src, dst, half):
        each(n_inner, lambda k: inner_copy(stage + half, k, src, dst, half_rows(half)).wait_send())

    def keep_inner(src, dst, half):
        at = half_rows(half)
        dst[inner, at, :] = src[inner, at, :]

    def send_low(stage, src, dst, half):
        each(n_low, lambda k: low_copy(stage + half, k, src, dst, half).start())
        dst[half, low] = src[half, low]

    def recv_low(stage, src, dst, half):
        each(n_low, lambda k: low_copy(stage + half, k, src, dst, half).wait_recv())

    def sent_low(stage, src, dst, half):
        each(n_low, lambda k: low_copy(stage + half, k, src, dst, half).wait_send())

    def send_high(stage, src, dst, half):
        each(n_high, lambda k: high_copy(stage + half, k, src, dst, half).start())
        dst[half, high] = src[half]

    def recv_high(stage, src, dst, half):
        each(n_high, lambda k: high_copy(stage + half, k, src, dst, half).wait_recv())

    def sent_high(stage, src, dst, half):
        each(n_high, lambda k: high_copy(stage + half, k, src, dst, half).wait_send())

    def factor1(e, head):
        return jnp.exp(total1[e, pl.ds(head, 1), :])

    def factor2(e, half):
        return jnp.exp(total2[e, pl.ds(half * ratio + low, 1), :])

    def factor3(e, half):
        return jnp.exp(total3[e, pl.ds(half * ratio + low, 1), :])

    def head_rows(head):
        return pl.ds(pl.multiple_of(head * width, width), width)

    def fold_gains(half):
        def body(r, none):
            head = half * ratio + r
            at = head_rows(head)
            value = gain1[0, at, :].astype(F32)
            for e in range(1, n_inner):
                value = factor1(e, head) * value + gain1[e, at, :].astype(F32)
            send_gain2[half, r] = value.astype(BF16)
            return none

        lax.fori_loop(0, ratio, body, 0)

    def fold_owns(half):
        def body(r, none):
            head = half * ratio + r
            at = head_rows(head)
            value = own1[n_inner - 1, at, :].astype(F32)
            for e in range(n_inner - 2, -1, -1):
                value = factor1(e, head) * value + own1[e, at, :].astype(F32)
            send_own2[half, r] = value.astype(BF16)
            return none

        lax.fori_loop(0, ratio, body, 0)

    def fold_gains2(half):
        value = gain2[half, 0].astype(F32)
        for e in range(1, n_low):
            value = factor2(e, half) * value + gain2[half, e].astype(F32)
        send_gain3[half] = value.astype(BF16)

    def fold_owns2(half):
        value = own2[half, n_low - 1].astype(F32)
        for e in range(n_low - 2, -1, -1):
            value = factor2(e, half) * value + own2[half, e].astype(F32)
        send_own3[half] = value.astype(BF16)

    def spread_states(half):
        value = init_ref[half]
        for e in range(n_high - 1):
            later = factor3(e, half) * value + gain3[half, e].astype(F32)
            value = jnp.where(e < high, later, value)
        for e in range(n_low):
            send_before[half, e] = value.astype(BF16)
            if e < n_low - 1:
                value = factor2(e, half) * value + gain2[half, e].astype(F32)

    def spread_afters(half):
        value = jnp.zeros(init_ref.shape[1:], F32)
        first = value
        for e in range(n_high - 1, -1, -1):
            first = factor3(e, half) * first + own3[half, e].astype(F32)
            value = jnp.where(e > high, first, value)
        first = first.astype(BF16)
        for e in range(n_low - 1, -1, -1):
            send_behind[half, e, 0:width] = value.astype(BF16)
            send_behind[half, e, width:] = first
            if e > 0:
                value = factor2(e, half) * value + own2[half, e].astype(F32)

    def fill_states(half):
        def body(r, none):
            head = half * ratio + r
            at = head_rows(head)
            value = before[half, r].astype(F32)
            for e in range(n_inner):
                send_state[e, at, :] = value.astype(BF16)
                if e < n_inner - 1:
                    value = factor1(e, head) * value + gain1[e, at, :].astype(F32)
            return none

        lax.fori_loop(0, ratio, body, 0)
        keep_inner(send_state, state_ref, half)

    def fill_afters(half):
        def body(r, none):
            head = half * ratio + r
            at = head_rows(head)
            start_ref[at, :] = behind[half, r, width:].astype(F32)
            value = behind[half, r, 0:width].astype(F32)
            for e in range(n_inner - 1, -1, -1):
                send_after[e, at, :] = value.astype(BF16)
                if e > 0:
                    value = factor1(e, head) * value + own1[e, at, :].astype(F32)
            return none

        lax.fori_loop(0, ratio, body, 0)
        keep_inner(send_after, after_ref, half)

    gains, owns = (1, send_gain, gain1), (3, send_own, own1)
    states, afters = (5, send_state, state_ref), (7, send_after, after_ref)
    gains2, owns2 = (1, send_gain2, gain2), (3, send_own2, own2)
    befores, behinds = (5, send_before, before), (7, send_behind, behind)
    gains3, owns3 = (1, send_gain3, gain3), (3, send_own3, own3)

    loads[0].wait()
    loads[1].wait()
    send_gains(0)
    send_gains(1)

    each(n_inner, lambda k: total_copy(k).wait_recv())
    row = total1[0]
    for e in range(1, n_inner):
        row = row + total1[e]
    send_total2[...] = row
    each(n_low, lambda k: total2_copy(k).start())
    total2[low] = row

    loads[2].wait()
    loads[3].wait()
    fill_owns(0)
    fill_owns(1)

    each(n_low, lambda k: total2_copy(k).wait_recv())
    row = total2[0]
    for e in range(1, n_low):
        row = row + total2[e]
    send_total3[...] = row
    each(n_high, lambda k: total3_copy(k).start())
    total3[high] = row

    up_sum[...] = jnp.zeros_like(up_sum)
    low_sum[...] = jnp.zeros_like(low_sum)

    recv_inner(*gains, 0)
    fold_gains(0)
    send_low(*gains2, 0)
    local_parts(0, 1)
    recv_low(*gains2, 0)
    fold_gains2(0)
    send_high(*gains3, 0)
    sent_inner(*gains, 0)
    sent_inner(*gains, 1)
    send_inner(*owns, 0)
    each(n_high, lambda k: total3_copy(k).wait_recv())
    loads[4].wait()
    loads[5].wait()
    recv_inner(*gains, 1)
    fold_gains(1)
    send_low(*gains2, 1)
    recv_high(*gains3, 0)
    spread_states(0)
    send_low(*befores, 0)
    local_parts(1, 2)
    recv_low(*gains2, 1)
    fold_gains2(1)
    send_high(*gains3, 1)
    sent_inner(*owns, 0)
    send_inner(*owns, 1)
    recv_high(*gains3, 1)
    spread_states(1)
    send_low(*befores, 1)
    recv_inner(*owns, 0)
    fold_owns(0)
    send_low(*owns2, 0)
    recv_low(*befores, 0)
    fill_states(0)
    recv_low(*owns2, 0)
    fold_owns2(0)
    send_high(*owns3, 0)
    recv_low(*befores, 1)
    fill_states(1)
    sent_inner(*owns, 1)
    send_inner(*states, 0)
    recv_inner(*owns, 1)
    fold_owns(1)
    send_low(*owns2, 1)
    recv_high(*owns3, 0)
    spread_afters(0)
    send_low(*behinds, 0)
    local_parts(2, 3)
    recv_low(*owns2, 1)
    fold_owns2(1)
    send_high(*owns3, 1)
    sent_inner(*states, 0)
    send_inner(*states, 1)
    recv_high(*owns3, 1)
    spread_afters(1)
    send_low(*behinds, 1)
    recv_low(*behinds, 0)
    fill_afters(0)
    local_parts(3, 6)
    sent_inner(*states, 1)
    send_inner(*afters, 0)
    recv_low(*behinds, 1)
    fill_afters(1)
    store_start = store(0, start_ref, dstart_hbm)
    store_start.start()
    local_parts(6, 8)
    parts(states, 0, state_part)
    sent_inner(*afters, 0)
    send_inner(*afters, 1)
    parts(states, 1, state_part)
    stores = [store(1, y_ref, y_hbm), store(2, dout_ref, dout_hbm)]
    for copy in stores:
        copy.start()

    each(n_inner, lambda k: total_copy(k).wait_send())
    each(n_low, lambda k: total2_copy(k).wait_send())
    each(n_high, lambda k: total3_copy(k).wait_send())
    for half in range(2):
        for stage in (gains2, owns2, befores, behinds):
            sent_low(*stage, half)
        for stage in (gains3, owns3):
            sent_high(*stage, half)
    parts(afters, 0, after_part)
    sent_inner(*afters, 1)
    parts(afters, 1, after_part)

    row = iota((length, length), 0)
    column = iota((length, length), 1)
    ddecay_ref[...] = (
        exact_dot(up_sum[...], jnp.where(row >= column, 1.0, 0.0), TN)
        + exact_dot(low_sum[...], jnp.where(row < column, 1.0, 0.0), TN)
        + jnp.sum(state_sum[...], axis=1, keepdims=True)
    ).astype(BF16)
    ends = [store(3, dx_ref, dx_hbm), store(4, din_ref, din_hbm), store(5, ddecay_ref, ddecay_hbm)]
    for copy in ends:
        copy.start()
    for copy in [store_start] + stores + ends:
        copy.wait()


def carry(x, decay, read_in, read_out, grad, init, n_outer, n_inner, width, depth):
    length = x.shape[0]
    groups = read_in.shape[1] // depth
    heads = decay.shape[0]
    ratio = heads // groups
    mine = heads // n_inner
    n_low = ratio
    n_high = n_outer // n_low
    vmem = pl.BlockSpec(memory_space=pltpu.VMEM)
    hbm = pl.BlockSpec(memory_space=pl.ANY)
    chunks = pltpu.VMEM((n_inner, mine * width, depth), BF16)
    runs = pltpu.VMEM((2, n_low, width, depth), BF16)
    doubles = pltpu.VMEM((2, n_low, 2 * width, depth), BF16)
    head = pltpu.VMEM((2, width, depth), BF16)
    highs = pltpu.VMEM((2, n_high, width, depth), BF16)
    total = pltpu.VMEM((mine, depth), F32)
    wide = jax.ShapeDtypeStruct(x.shape, BF16)
    narrow = jax.ShapeDtypeStruct(read_in.shape, BF16)
    wide32 = pltpu.VMEM(x.shape, F32)
    narrow32 = pltpu.VMEM(read_in.shape, F32)
    dma = pltpu.SemaphoreType.DMA
    return pl.pallas_call(
        functools.partial(carry_kernel, n_inner, n_low, n_high, ratio, width),
        in_specs=[hbm, vmem, hbm, hbm, hbm, hbm],
        out_specs=[hbm] * 6,
        out_shape=[
            wide,
            wide,
            jax.ShapeDtypeStruct(decay.shape, BF16),
            narrow,
            narrow,
            jax.ShapeDtypeStruct((mine * width, depth), F32),
        ],
        scratch_shapes=[
            chunks,
            chunks,
            pltpu.VMEM((mine * width, depth), F32),
            wide32,
            wide32,
            pltpu.VMEM(x.shape, BF16),
            pltpu.VMEM(x.shape, BF16),
            wide32,
            wide32,
            narrow32,
            narrow32,
            pltpu.VMEM((length, heads), F32),
            pltpu.VMEM((length, heads), F32),
            pltpu.VMEM((heads, depth), F32),
            pltpu.VMEM(x.shape, BF16),
            pltpu.VMEM(x.shape, BF16),
            pltpu.VMEM(decay.shape, BF16),
            pltpu.VMEM(read_in.shape, BF16),
            pltpu.VMEM(read_out.shape, BF16),
            pltpu.VMEM(x.shape, BF16),
            pltpu.VMEM(read_in.shape, BF16),
            pltpu.VMEM(read_out.shape, BF16),
            pltpu.VMEM(grad.shape, BF16),
            pltpu.VMEM((2, width, depth), F32),
            pltpu.VMEM((n_inner, mine, depth), F32),
            pltpu.VMEM((n_inner, mine, depth), F32),
            total,
            pltpu.VMEM((n_low, mine, depth), F32),
            total,
            pltpu.VMEM((n_high, mine, depth), F32),
            chunks,
            chunks,
            chunks,
            chunks,
            runs,
            runs,
            runs,
            runs,
            head,
            highs,
            head,
            highs,
            runs,
            runs,
            doubles,
            doubles,
            chunks,
            chunks,
            dma((6,)),
            dma((6,)),
            dma((9, n_inner)),
            dma((9, n_inner)),
            dma((9, n_low)),
            dma((9, n_low)),
            dma((5, n_high)),
            dma((5, n_high)),
        ],
        compiler_params=pltpu.CompilerParams(
            collective_id=0, has_side_effects=True, vmem_limit_bytes=60 * 2**20
        ),
        name="carry",
    )(x, decay, read_in, read_out, grad, init)


def deliver_kernel(*refs):
    n = (len(refs) - 2) // 3
    hbm, out, held, (loaded, stored) = refs[:n], refs[n : 2 * n], refs[2 * n : 3 * n], refs[3 * n :]
    loads = [pltpu.make_async_copy(hbm[i], held[i], loaded.at[i]) for i in range(n)]
    stores = [pltpu.make_async_copy(held[i], out[i], stored.at[i]) for i in range(n)]
    for load in loads:
        load.start()
    for load, store in zip(loads, stores):
        load.wait()
        store.start()
    for store in stores:
        store.wait()


def deliver(*arrays):
    n = len(arrays)
    hbm = pl.BlockSpec(memory_space=pl.ANY)
    return pl.pallas_call(
        deliver_kernel,
        in_specs=[hbm] * n,
        out_specs=[hbm] * n,
        out_shape=[jax.ShapeDtypeStruct(a.shape, a.dtype) for a in arrays],
        scratch_shapes=[pltpu.VMEM(a.shape, a.dtype) for a in arrays]
        + [pltpu.SemaphoreType.DMA((n,))] * 2,
        compiler_params=pltpu.CompilerParams(vmem_limit_bytes=60 * 2**20),
        name="deliver",
    )(*arrays)


def shards(inputs, log_decay, read_in, read_out, initial_state, output_grad):
    n_outer, n_inner = lax.axis_size("outer"), lax.axis_size("inner")
    width, depth = initial_state.shape[1:]
    decay = log_decay.T
    results = carry(
        inputs,
        decay,
        read_in,
        read_out,
        output_grad,
        initial_state.reshape(-1, depth),
        n_outer,
        n_inner,
        width,
        depth,
    )
    y, dx, ddecay, din, dout, dstart = deliver(*results)
    return (y, dx, ddecay.T, din, dout, dstart.reshape(initial_state.shape))


def solution(mesh):
    tokens = P(("outer", "inner"), None)
    held = P("inner", None, None)
    return jax.shard_map(
        shards,
        mesh=mesh,
        in_specs=(tokens, tokens, tokens, tokens, held, tokens),
        out_specs=(tokens, tokens, tokens, tokens, tokens, held),
        check_vma=False,
    )
```

```python
import functools

import jax
import jax.numpy as jnp
from jax import lax
from jax.experimental import pallas as pl
from jax.experimental.pallas import tpu as pltpu
from jax.sharding import PartitionSpec as P

F32 = jnp.float32
BF16 = jnp.bfloat16
NN = ((1,), (0,))
NT = ((1,), (1,))
TN = ((0,), (0,))
MESH = pl.DeviceIdType.MESH


def dot(a, b, dims):
    return lax.dot_general(a, b, (dims, ((), ())), preferred_element_type=F32)


def exact_dot(a, b, dims):
    return lax.dot_general(
        a, b, (dims, ((), ())), preferred_element_type=F32, precision=lax.Precision.HIGHEST
    )


def split_dot(a, b, dims):
    high = a.astype(BF16)
    low = (a - high.astype(F32)).astype(BF16)
    return dot(high, b, dims) + dot(low, b, dims)


def iota(shape, axis):
    return lax.broadcasted_iota(jnp.int32, shape, axis)


def as_bf16(mask):
    return jnp.where(mask, 1.0, 0.0).astype(BF16)


def lower(length):
    return as_bf16(iota((length, length), 0) >= iota((length, length), 1))


def spread_sums(decay_ref, group, ratio, width):
    heads, length = decay_ref.shape
    columns = ratio * width
    pick = as_bf16(iota((heads, columns), 0) == group * ratio + iota((heads, columns), 1) // width)
    return dot(lower(length), dot(decay_ref[...], pick, TN).astype(BF16), NN)


def head_decays(decay_ref, group, ratio):
    heads, length = decay_ref.shape
    pick = as_bf16(iota((ratio, heads), 1) == group * ratio + iota((ratio, heads), 0))
    return dot(pick, decay_ref[...], NN).astype(BF16)


def carry_kernel(
    n_inner,
    n_low,
    n_high,
    ratio,
    width,
    x_hbm,
    decay_ref,
    in_hbm,
    out_hbm,
    grad_hbm,
    init_hbm,
    y_hbm,
    dx_hbm,
    ddecay_hbm,
    din_hbm,
    dout_hbm,
    dstart_hbm,
    state_ref,
    after_ref,
    start_ref,
    from_start,
    to_end,
    weighted_ref,
    scaled_ref,
    y_sum,
    dx_sum,
    din_sum,
    dout_sum,
    up_sum,
    low_sum,
    state_sum,
    y_ref,
    dx_ref,
    ddecay_ref,
    din_ref,
    dout_ref,
    x_ref,
    in_ref,
    out_ref,
    grad_ref,
    init_ref,
    send_total,
    total1,
    send_total2,
    total2,
    send_total3,
    total3,
    send_gain,
    gain1,
    send_own,
    own1,
    send_gain2,
    gain2,
    send_own2,
    own2,
    send_gain3,
    gain3,
    send_own3,
    own3,
    send_before,
    before,
    send_behind,
    behind,
    send_first,
    firsts,
    send_state,
    send_after,
    load_sem,
    store_sem,
    inner_send,
    inner_recv,
    low_send,
    low_recv,
    high_send,
    high_recv,
    ready,
):
    outer = lax.axis_index("outer")
    inner = lax.axis_index("inner")
    low = lax.rem(outer, n_low)
    high = lax.div(outer, n_low)
    length = x_ref.shape[0]
    depth = in_ref.shape[1] * ratio // decay_ref.shape[0]
    columns = ratio * width

    def around(here, k, n):
        there = here + k
        return jnp.where(there >= n, there - n, there)

    def inner_peer(k):
        return around(inner, k, n_inner)

    def low_peer(k):
        return around(low, k, n_low)

    def high_peer(k):
        return around(high, k, n_high)

    def inner_id(k):
        return (outer, inner_peer(k))

    def low_id(k):
        return (high * n_low + low_peer(k), inner)

    def high_id(k):
        return (high_peer(k) * n_low + low, inner)

    def each(n, act):
        def body(k, none):
            act(k)
            return none

        lax.fori_loop(1, n, body, 0)

    def unrolled(n, act):
        for k in range(1, n):
            act(k)

    def remote(src, dst, send, recv, to):
        return pltpu.make_async_remote_copy(
            src_ref=src,
            dst_ref=dst,
            send_sem=send,
            recv_sem=recv,
            device_id=to,
            device_id_type=MESH,
        )

    def inner_copy(stage, k, src, dst, at=slice(None)):
        return remote(
            src.at[inner_peer(k), at],
            dst.at[inner, at],
            inner_send.at[stage, k],
            inner_recv.at[stage, k],
            inner_id(k),
        )

    def low_copy(stage, k, src, dst, half):
        return remote(
            src.at[half, low_peer(k)],
            dst.at[half, low],
            low_send.at[stage, k],
            low_recv.at[stage, k],
            low_id(k),
        )

    def high_copy(stage, k, src, dst, half):
        return remote(
            src.at[half],
            dst.at[half, high],
            high_send.at[stage, k],
            high_recv.at[stage, k],
            high_id(k),
        )

    def first_copy(half, k):
        return remote(
            send_first.at[half],
            firsts.at[half, low],
            low_send.at[9 + half, k],
            low_recv.at[9 + half, k],
            low_id(k),
        )

    def total_copy(k):
        return remote(
            send_total.at[inner_peer(k)],
            total1.at[inner],
            inner_send.at[0, k],
            inner_recv.at[0, k],
            inner_id(k),
        )

    def total2_copy(k):
        return remote(
            send_total2, total2.at[low], low_send.at[0, k], low_recv.at[0, k], low_id(k)
        )

    def total3_copy(k):
        return remote(
            send_total3, total3.at[high], high_send.at[0, k], high_recv.at[0, k], high_id(k)
        )

    loads = [
        pltpu.make_async_copy(src, dst, load_sem.at[i])
        for i, (src, dst) in enumerate(
            ((x_hbm, x_ref), (in_hbm, in_ref), (grad_hbm, grad_ref), (out_hbm, out_ref))
        )
    ]
    for half in range(2):
        rows = pl.ds(pl.multiple_of((half * ratio + low) * width, width), width)
        loads.append(
            pltpu.make_async_copy(init_hbm.at[rows], init_ref.at[half], load_sem.at[4 + half])
        )
    for load in loads:
        load.start()

    barrier = pltpu.get_barrier_semaphore()
    for n, peer in ((n_inner, inner_id), (n_low, low_id), (n_high, high_id)):
        unrolled(
            n,
            lambda k, peer=peer: pl.semaphore_signal(
                barrier, inc=1, device_id=peer(k), device_id_type=MESH
            ),
        )

    def send_totals():
        totals = dot(decay_ref[...], jnp.ones((length, send_total.shape[2]), BF16), NN)
        for e in range(n_inner):
            send_total[e] = totals[e * 2 * ratio : (e + 1) * 2 * ratio]
        unrolled(n_inner, lambda k: total_copy(k).start())
        total1[inner] = send_total[inner]

    def half_rows(half):
        return pl.ds(half * columns, columns)

    def group_slices(group):
        return (
            pl.ds(pl.multiple_of(group * columns, columns), columns),
            pl.ds(pl.multiple_of(group * depth, depth), depth),
        )

    def gain_of(half, k):
        group = 2 * inner_peer(k) + half
        wide, narrow = group_slices(group)
        summed = spread_sums(decay_ref, group, ratio, width)
        from_start[:, wide] = jnp.exp(summed)
        factor = jnp.exp(summed[length - 1 :] - summed)
        to_end[:, wide] = factor
        weighted = (x_ref[:, wide].astype(F32) * factor).astype(BF16)
        weighted_ref[:, wide] = weighted
        return dot(weighted, in_ref[:, narrow], TN).astype(BF16)

    def own_of(half, k):
        wide, narrow = group_slices(2 * inner_peer(k) + half)
        scaled = (grad_ref[:, wide].astype(F32) * from_start[:, wide]).astype(BF16)
        scaled_ref[:, wide] = scaled
        return dot(scaled, out_ref[:, narrow], TN).astype(BF16)

    def local_part(group):
        wide, narrow = group_slices(group)
        picked = head_decays(decay_ref, group, ratio)
        below = lower(length)
        down = dot(below, picked, NT)
        across = dot(picked, below, NT)
        x, grad = x_ref[:, wide], grad_ref[:, wide]
        b, c = in_ref[:, narrow], out_ref[:, narrow]
        scores = dot(c, b, NT)
        causal = iota((length, length), 0) >= iota((length, length), 1)
        ys, dxs = [], []
        dscores = jnp.zeros((length, length), F32)
        for r in range(ratio):
            gap = down[:, r : r + 1] - across[r : r + 1, :]
            decays = jnp.exp(jnp.where(causal, gap, -1e30))
            weights = (scores * decays).astype(BF16)
            at = slice(r * width, (r + 1) * width)
            ys.append(dot(weights, x[:, at], NN))
            dxs.append(dot(weights, grad[:, at], TN))
            dscores = dscores + dot(grad[:, at], x[:, at], NT) * decays
        y_sum[:, wide] = jnp.concatenate(ys, axis=1)
        dx_sum[:, wide] = jnp.concatenate(dxs, axis=1)
        dscores = dscores.astype(BF16)
        dout_sum[:, narrow] = dot(dscores, b, NN)
        din_sum[:, narrow] = dot(dscores, c, TN)

    def place(group):
        heads = decay_ref.shape[0]
        head = group * ratio + iota((columns, heads), 0) // width
        return as_bf16(iota((columns, heads), 1) == head)

    def state_part(half, k):
        owner = around(inner, n_inner - k, n_inner)
        group = 2 * owner + half
        wide, narrow = group_slices(group)
        state = state_ref[owner, half_rows(half), :]
        y = y_sum[:, wide] + dot(out_ref[:, narrow], state, NT) * from_start[:, wide]
        y_ref[:, wide] = y.astype(BF16)
        dout = dout_sum[:, narrow] + dot(scaled_ref[:, wide], state, NN)
        dout_ref[:, narrow] = dout.astype(BF16)
        change = y * grad_ref[:, wide].astype(F32) - x_ref[:, wide].astype(F32) * dx_sum[:, wide]
        up_sum[...] += split_dot(change, place(group), NN)

    def part_stores(half, k):
        wide, narrow = group_slices(2 * around(inner, n_inner - k, n_inner) + half)
        return (
            store(4 + 2 * (half * n_inner + k), dx_ref.at[:, wide], dx_hbm.at[:, wide]),
            store(5 + 2 * (half * n_inner + k), din_ref.at[:, narrow], din_hbm.at[:, narrow]),
        )

    def after_part(half, k):
        owner = around(inner, n_inner - k, n_inner)
        group = 2 * owner + half
        wide, narrow = group_slices(group)
        state = state_ref[owner, half_rows(half), :]
        after = after_ref[owner, half_rows(half), :]
        far = dot(in_ref[:, narrow], after, NT) * to_end[:, wide]
        dx_ref[:, wide] = (dx_sum[:, wide] + far).astype(BF16)
        din = din_sum[:, narrow] + dot(weighted_ref[:, wide], after, NN)
        din_ref[:, narrow] = din.astype(BF16)
        low_sum[...] += split_dot(x_ref[:, wide].astype(F32) * far, place(group), NN)
        product = state.astype(F32) * after.astype(F32)
        picked = head_decays(decay_ref, group, ratio)
        total = dot(picked, jnp.ones((length, depth), BF16), NN)
        state_sum[pl.ds(pl.multiple_of(group * ratio, ratio), ratio), :] = jnp.sum(
            product.reshape(ratio, width, depth), axis=1
        ) * jnp.exp(total)
        for copy in part_stores(half, k):
            copy.start()

    def local_parts(start, stop):
        def body(group, none):
            local_part(group)
            return none

        groups = n_inner * 2
        lax.fori_loop(start * groups // 8, stop * groups // 8, body, 0)

    def parts(stage, half, part):
        part(half, 0)

        def act(k):
            inner_copy(stage[0] + half, k, stage[1], stage[2], half_rows(half)).wait_recv()
            part(half, k)

        each(n_inner, act)

    def store(i, src, dst):
        return pltpu.make_async_copy(src, dst, store_sem.at[i])

    def fill_gains(half, go):
        at = half_rows(half)

        def act(k):
            send_gain[inner_peer(k), at, :] = gain_of(half, k)
            if go:
                inner_copy(1 + half, k, send_gain, gain1, at).start()

        each(n_inner, act)
        gain1[inner, at, :] = gain_of(half, 0)

    def fill_owns(half):
        at = half_rows(half)

        def act(k):
            send_own[inner_peer(k), at, :] = own_of(half, k)

        each(n_inner, act)
        own1[inner, at, :] = own_of(half, 0)

    def send_inner(stage, src, dst, half):
        unrolled(n_inner, lambda k: inner_copy(stage + half, k, src, dst, half_rows(half)).start())

    def recv_inner(stage, src, dst, half):
        unrolled(n_inner, lambda k: inner_copy(stage + half, k, src, dst, half_rows(half)).wait_recv())

    def sent_inner(stage, src, dst, half):
        unrolled(n_inner, lambda k: inner_copy(stage + half, k, src, dst, half_rows(half)).wait_send())

    def keep_inner(src, dst, half):
        at = half_rows(half)
        dst[inner, at, :] = src[inner, at, :]

    def send_low(stage, src, dst, half):
        unrolled(n_low, lambda k: low_copy(stage + half, k, src, dst, half).start())
        dst[half, low] = src[half, low]

    def recv_low(stage, src, dst, half):
        unrolled(n_low, lambda k: low_copy(stage + half, k, src, dst, half).wait_recv())

    def sent_low(stage, src, dst, half):
        unrolled(n_low, lambda k: low_copy(stage + half, k, src, dst, half).wait_send())

    def send_high(stage, src, dst, half):
        unrolled(n_high, lambda k: high_copy(stage + half, k, src, dst, half).start())
        dst[half, high] = src[half]

    def recv_high(stage, src, dst, half):
        unrolled(n_high, lambda k: high_copy(stage + half, k, src, dst, half).wait_recv())

    def sent_high(stage, src, dst, half):
        unrolled(n_high, lambda k: high_copy(stage + half, k, src, dst, half).wait_send())

    def factor1(e, head):
        return jnp.exp(total1[e, pl.ds(head, 1), :])

    def factor2(e, half):
        return jnp.exp(total2[e, pl.ds(half * ratio + low, 1), :])

    def factor3(e, half):
        return jnp.exp(total3[e, pl.ds(half * ratio + low, 1), :])

    def head_rows(head):
        return pl.ds(pl.multiple_of(head * width, width), width)

    def fold_gains(half):
        def body(r, none):
            head = half * ratio + r
            at = head_rows(head)
            value = gain1[0, at, :].astype(F32)
            for e in range(1, n_inner):
                value = factor1(e, head) * value + gain1[e, at, :].astype(F32)
            send_gain2[half, r] = value.astype(BF16)
            return none

        lax.fori_loop(0, ratio, body, 0)

    def fold_owns(half):
        def body(r, none):
            head = half * ratio + r
            at = head_rows(head)
            value = own1[n_inner - 1, at, :].astype(F32)
            for e in range(n_inner - 2, -1, -1):
                value = factor1(e, head) * value + own1[e, at, :].astype(F32)
            send_own2[half, r] = value.astype(BF16)
            return none

        lax.fori_loop(0, ratio, body, 0)

    def fold_gains2(half):
        value = gain2[half, 0].astype(F32)
        for e in range(1, n_low):
            value = factor2(e, half) * value + gain2[half, e].astype(F32)
        send_gain3[half] = value.astype(BF16)

    def fold_owns2(half):
        value = own2[half, n_low - 1].astype(F32)
        for e in range(n_low - 2, -1, -1):
            value = factor2(e, half) * value + own2[half, e].astype(F32)
        send_own3[half] = value.astype(BF16)

    def spread_states(half):
        value = init_ref[half]
        for e in range(n_high - 1):
            later = factor3(e, half) * value + gain3[half, e].astype(F32)
            value = jnp.where(e < high, later, value)
        for e in range(n_low):
            send_before[half, e] = value.astype(BF16)
            if e < n_low - 1:
                value = factor2(e, half) * value + gain2[half, e].astype(F32)

    def spread_afters(half):
        value = jnp.zeros(init_ref.shape[1:], F32)
        first = value
        for e in range(n_high - 1, -1, -1):
            first = factor3(e, half) * first + own3[half, e].astype(F32)
            value = jnp.where(e > high, first, value)
        send_first[half] = first.astype(BF16)
        for e in range(n_low - 1, -1, -1):
            send_behind[half, e] = value.astype(BF16)
            if e > 0:
                value = factor2(e, half) * value + own2[half, e].astype(F32)

    def fill_states(half):
        def body(r, none):
            head = half * ratio + r
            at = head_rows(head)
            value = before[half, r].astype(F32)
            for e in range(n_inner):
                send_state[e, at, :] = value.astype(BF16)
                if e < n_inner - 1:
                    value = factor1(e, head) * value + gain1[e, at, :].astype(F32)
            return none

        lax.fori_loop(0, ratio, body, 0)
        keep_inner(send_state, state_ref, half)

    def fill_afters(half):
        def body(r, none):
            head = half * ratio + r
            at = head_rows(head)
            value = behind[half, r].astype(F32)
            for e in range(n_inner - 1, -1, -1):
                send_after[e, at, :] = value.astype(BF16)
                if e > 0:
                    value = factor1(e, head) * value + own1[e, at, :].astype(F32)
            return none

        lax.fori_loop(0, ratio, body, 0)
        keep_inner(send_after, after_ref, half)

    def send_firsts(half):
        unrolled(n_low, lambda k: first_copy(half, k).start())
        firsts[half, low] = send_first[half]

    def put_firsts(half):
        unrolled(n_low, lambda k: first_copy(half, k).wait_recv())
        for r in range(ratio):
            start_ref[pl.ds((half * ratio + r) * width, width), :] = firsts[half, r].astype(F32)

    gains, owns = (1, send_gain, gain1), (3, send_own, own1)
    states, afters = (5, send_state, state_ref), (7, send_after, after_ref)
    gains2, owns2 = (1, send_gain2, gain2), (3, send_own2, own2)
    befores, behinds = (5, send_before, before), (7, send_behind, behind)
    gains3, owns3 = (1, send_gain3, gain3), (3, send_own3, own3)

    up_sum[...] = jnp.zeros_like(up_sum)
    low_sum[...] = jnp.zeros_like(low_sum)
    loads[0].wait()
    loads[1].wait()
    fill_gains(0, False)
    pl.semaphore_wait(barrier, n_inner + n_low + n_high - 3)
    send_totals()
    send_inner(*gains, 0)
    fill_gains(1, True)
    loads[2].wait()
    loads[3].wait()
    fill_owns(0)

    unrolled(n_inner, lambda k: total_copy(k).wait_recv())
    row = total1[0]
    for e in range(1, n_inner):
        row = row + total1[e]
    send_total2[...] = row
    total2[low] = row
    unrolled(n_low, lambda k: total2_copy(k).start())
    fill_owns(1)
    local_parts(0, 2)

    unrolled(n_low, lambda k: total2_copy(k).wait_recv())
    row = total2[0]
    for e in range(1, n_low):
        row = row + total2[e]
    send_total3[...] = row
    total3[high] = row
    unrolled(n_high, lambda k: total3_copy(k).start())
    recv_inner(*gains, 0)
    fold_gains(0)
    send_low(*gains2, 0)
    send_inner(*owns, 0)
    local_parts(2, 6)
    recv_low(*gains2, 0)
    fold_gains2(0)
    send_high(*gains3, 0)
    recv_inner(*gains, 1)
    fold_gains(1)
    send_low(*gains2, 1)
    send_inner(*owns, 1)
    local_parts(6, 8)
    loads[4].wait()
    loads[5].wait()
    unrolled(n_high, lambda k: total3_copy(k).wait_recv())
    recv_high(*gains3, 0)
    spread_states(0)
    send_low(*befores, 0)
    recv_low(*gains2, 1)
    fold_gains2(1)
    send_high(*gains3, 1)
    recv_inner(*owns, 0)
    fold_owns(0)
    send_low(*owns2, 0)
    recv_low(*befores, 0)
    fill_states(0)
    send_inner(*states, 0)
    recv_high(*gains3, 1)
    spread_states(1)
    send_low(*befores, 1)
    recv_low(*owns2, 0)
    fold_owns2(0)
    send_high(*owns3, 0)
    recv_inner(*owns, 1)
    fold_owns(1)
    send_low(*owns2, 1)
    recv_low(*befores, 1)
    fill_states(1)
    send_inner(*states, 1)
    recv_high(*owns3, 0)
    spread_afters(0)
    send_low(*behinds, 0)
    send_firsts(0)
    recv_low(*owns2, 1)
    fold_owns2(1)
    send_high(*owns3, 1)
    parts(states, 0, state_part)
    recv_low(*behinds, 0)
    fill_afters(0)
    send_inner(*afters, 0)
    recv_high(*owns3, 1)
    spread_afters(1)
    send_low(*behinds, 1)
    send_firsts(1)
    parts(states, 1, state_part)
    recv_low(*behinds, 1)
    fill_afters(1)
    send_inner(*afters, 1)
    put_firsts(0)
    put_firsts(1)
    for half in range(2):
        unrolled(n_low, lambda k, half=half: first_copy(half, k).wait_send())
    store_start = store(0, start_ref, dstart_hbm)
    store_start.start()
    stores = [store(1, y_ref, y_hbm), store(2, dout_ref, dout_hbm)]
    for copy in stores:
        copy.start()

    unrolled(n_inner, lambda k: total_copy(k).wait_send())
    unrolled(n_low, lambda k: total2_copy(k).wait_send())
    unrolled(n_high, lambda k: total3_copy(k).wait_send())
    for half in range(2):
        for stage in (gains2, owns2, befores, behinds):
            sent_low(*stage, half)
        for stage in (gains3, owns3):
            sent_high(*stage, half)
        for stage in (gains, owns, states):
            sent_inner(*stage, half)
    row = iota((length, length), 0)
    column = iota((length, length), 1)
    up_total = exact_dot(up_sum[...], jnp.where(row >= column, 1.0, 0.0), TN)
    parts(afters, 0, after_part)
    parts(afters, 1, after_part)
    sent_inner(*afters, 0)
    sent_inner(*afters, 1)

    ddecay_ref[...] = (
        up_total
        + exact_dot(low_sum[...], jnp.where(row < column, 1.0, 0.0), TN)
        + jnp.sum(state_sum[...], axis=1, keepdims=True)
    ).astype(BF16)
    end = store(3, ddecay_ref, ddecay_hbm)
    end.start()
    for copy in [store_start] + stores + [end]:
        copy.wait()
    for half in range(2):
        for k in range(n_inner):
            for copy in part_stores(half, k):
                copy.wait()


def carry(x, decay, read_in, read_out, grad, init, n_outer, n_inner, width, depth):
    length = x.shape[0]
    groups = read_in.shape[1] // depth
    heads = decay.shape[0]
    ratio = heads // groups
    mine = heads // n_inner
    n_low = ratio
    n_high = n_outer // n_low
    vmem = pl.BlockSpec(memory_space=pltpu.VMEM)
    hbm = pl.BlockSpec(memory_space=pl.ANY)
    chunks = pltpu.VMEM((n_inner, mine * width, depth), BF16)
    runs = pltpu.VMEM((2, n_low, width, depth), BF16)
    head = pltpu.VMEM((2, width, depth), BF16)
    highs = pltpu.VMEM((2, n_high, width, depth), BF16)
    total = pltpu.VMEM((mine, depth), F32)
    wide = jax.ShapeDtypeStruct(x.shape, BF16)
    narrow = jax.ShapeDtypeStruct(read_in.shape, BF16)
    wide32 = pltpu.VMEM(x.shape, F32)
    narrow32 = pltpu.VMEM(read_in.shape, F32)
    dma = pltpu.SemaphoreType.DMA
    return pl.pallas_call(
        functools.partial(carry_kernel, n_inner, n_low, n_high, ratio, width),
        in_specs=[hbm, vmem, hbm, hbm, hbm, hbm],
        out_specs=[hbm] * 6,
        out_shape=[
            wide,
            wide,
            jax.ShapeDtypeStruct(decay.shape, BF16),
            narrow,
            narrow,
            jax.ShapeDtypeStruct((mine * width, depth), F32),
        ],
        scratch_shapes=[
            chunks,
            chunks,
            pltpu.VMEM((mine * width, depth), F32),
            wide32,
            wide32,
            pltpu.VMEM(x.shape, BF16),
            pltpu.VMEM(x.shape, BF16),
            wide32,
            wide32,
            narrow32,
            narrow32,
            pltpu.VMEM((length, heads), F32),
            pltpu.VMEM((length, heads), F32),
            pltpu.VMEM((heads, depth), F32),
            pltpu.VMEM(x.shape, BF16),
            pltpu.VMEM(x.shape, BF16),
            pltpu.VMEM(decay.shape, BF16),
            pltpu.VMEM(read_in.shape, BF16),
            pltpu.VMEM(read_out.shape, BF16),
            pltpu.VMEM(x.shape, BF16),
            pltpu.VMEM(read_in.shape, BF16),
            pltpu.VMEM(read_out.shape, BF16),
            pltpu.VMEM(grad.shape, BF16),
            pltpu.VMEM((2, width, depth), F32),
            pltpu.VMEM((n_inner, mine, depth), F32),
            pltpu.VMEM((n_inner, mine, depth), F32),
            total,
            pltpu.VMEM((n_low, mine, depth), F32),
            total,
            pltpu.VMEM((n_high, mine, depth), F32),
            chunks,
            chunks,
            chunks,
            chunks,
            runs,
            runs,
            runs,
            runs,
            head,
            highs,
            head,
            highs,
            runs,
            runs,
            runs,
            runs,
            head,
            runs,
            chunks,
            chunks,
            dma((6,)),
            dma((4 + 4 * n_inner,)),
            dma((9, n_inner)),
            dma((9, n_inner)),
            dma((11, n_low)),
            dma((11, n_low)),
            dma((5, n_high)),
            dma((5, n_high)),
            pltpu.SemaphoreType.REGULAR((2,)),
        ],
        compiler_params=pltpu.CompilerParams(
            collective_id=0, has_side_effects=True, vmem_limit_bytes=60 * 2**20
        ),
        name="carry",
    )(x, decay, read_in, read_out, grad, init)


def deliver_kernel(*refs):
    n = (len(refs) - 2) // 3
    hbm, out, held, (loaded, stored) = refs[:n], refs[n : 2 * n], refs[2 * n : 3 * n], refs[3 * n :]
    loads = [pltpu.make_async_copy(hbm[i], held[i], loaded.at[i]) for i in range(n)]
    stores = [pltpu.make_async_copy(held[i], out[i], stored.at[i]) for i in range(n)]
    for load in loads:
        load.start()
    for load, store in zip(loads, stores):
        load.wait()
        store.start()
    for store in stores:
        store.wait()


def deliver(*arrays):
    n = len(arrays)
    hbm = pl.BlockSpec(memory_space=pl.ANY)
    return pl.pallas_call(
        deliver_kernel,
        in_specs=[hbm] * n,
        out_specs=[hbm] * n,
        out_shape=[jax.ShapeDtypeStruct(a.shape, a.dtype) for a in arrays],
        scratch_shapes=[pltpu.VMEM(a.shape, a.dtype) for a in arrays]
        + [pltpu.SemaphoreType.DMA((n,))] * 2,
        compiler_params=pltpu.CompilerParams(vmem_limit_bytes=60 * 2**20),
        name="deliver",
    )(*arrays)


def shards(inputs, log_decay, read_in, read_out, initial_state, output_grad):
    n_outer, n_inner = lax.axis_size("outer"), lax.axis_size("inner")
    width, depth = initial_state.shape[1:]
    decay = log_decay.T
    results = carry(
        inputs,
        decay,
        read_in,
        read_out,
        output_grad,
        initial_state.reshape(-1, depth),
        n_outer,
        n_inner,
        width,
        depth,
    )
    y, dx, ddecay, din, dout, dstart = deliver(*results)
    return (y, dx, ddecay.T, din, dout, dstart.reshape(initial_state.shape))


def solution(mesh):
    tokens = P(("outer", "inner"), None)
    held = P("inner", None, None)
    return jax.shard_map(
        shards,
        mesh=mesh,
        in_specs=(tokens, tokens, tokens, tokens, held, tokens),
        out_specs=(tokens, tokens, tokens, tokens, tokens, held),
        check_vma=False,
    )
```

```python
import functools

import jax
import jax.numpy as jnp
from jax import lax
from jax.experimental import pallas as pl
from jax.experimental.pallas import tpu as pltpu
from jax.sharding import PartitionSpec as P

F32 = jnp.float32
BF16 = jnp.bfloat16
NN = ((1,), (0,))
NT = ((1,), (1,))
TN = ((0,), (0,))
MESH = pl.DeviceIdType.MESH


def dot(a, b, dims):
    return lax.dot_general(a, b, (dims, ((), ())), preferred_element_type=F32)


def exact_dot(a, b, dims):
    return lax.dot_general(
        a, b, (dims, ((), ())), preferred_element_type=F32, precision=lax.Precision.HIGHEST
    )


def split_dot(a, b, dims):
    high = a.astype(BF16)
    low = (a - high.astype(F32)).astype(BF16)
    return dot(high, b, dims) + dot(low, b, dims)


def iota(shape, axis):
    return lax.broadcasted_iota(jnp.int32, shape, axis)


def as_bf16(mask):
    return jnp.where(mask, 1.0, 0.0).astype(BF16)


def lower(length):
    return as_bf16(iota((length, length), 0) >= iota((length, length), 1))


def spread_sums(decay_ref, group, ratio, width):
    heads, length = decay_ref.shape
    columns = ratio * width
    pick = as_bf16(iota((heads, columns), 0) == group * ratio + iota((heads, columns), 1) // width)
    return dot(lower(length), dot(decay_ref[...], pick, TN).astype(BF16), NN)


def head_decays(decay_ref, group, ratio):
    heads, length = decay_ref.shape
    pick = as_bf16(iota((ratio, heads), 1) == group * ratio + iota((ratio, heads), 0))
    return dot(pick, decay_ref[...], NN).astype(BF16)


def carry_kernel(
    n_inner,
    n_low,
    n_high,
    ratio,
    width,
    x_hbm,
    decay_ref,
    in_hbm,
    out_hbm,
    grad_hbm,
    init_hbm,
    y_hbm,
    dx_hbm,
    ddecay_hbm,
    din_hbm,
    dout_hbm,
    dstart_hbm,
    state_ref,
    after_ref,
    start_ref,
    from_start,
    to_end,
    weighted_ref,
    scaled_ref,
    y_sum,
    dx_sum,
    din_sum,
    dout_sum,
    up_sum,
    low_sum,
    state_sum,
    y_ref,
    dx_ref,
    ddecay_ref,
    din_ref,
    dout_ref,
    x_ref,
    in_ref,
    out_ref,
    grad_ref,
    init_ref,
    send_total,
    total1,
    send_total2,
    total2,
    send_total3,
    total3,
    send_gain,
    gain1,
    send_own,
    own1,
    send_gain2,
    gain2,
    send_own2,
    own2,
    send_gain3,
    gain3,
    send_own3,
    own3,
    send_before,
    before,
    send_behind,
    behind,
    send_first,
    firsts,
    send_state,
    send_after,
    load_sem,
    store_sem,
    inner_send,
    inner_recv,
    low_send,
    low_recv,
    high_send,
    high_recv,
    ready,
):
    outer = lax.axis_index("outer")
    inner = lax.axis_index("inner")
    low = lax.rem(outer, n_low)
    high = lax.div(outer, n_low)
    length = x_ref.shape[0]
    depth = in_ref.shape[1] * ratio // decay_ref.shape[0]
    columns = ratio * width

    def around(here, k, n):
        there = here + k
        return jnp.where(there >= n, there - n, there)

    def inner_peer(k):
        return around(inner, k, n_inner)

    def low_peer(k):
        return around(low, k, n_low)

    def high_peer(k):
        return around(high, k, n_high)

    def inner_id(k):
        return (outer, inner_peer(k))

    def low_id(k):
        return (high * n_low + low_peer(k), inner)

    def high_id(k):
        return (high_peer(k) * n_low + low, inner)

    def each(n, act):
        def body(k, none):
            act(k)
            return none

        lax.fori_loop(1, n, body, 0)

    def unrolled(n, act):
        for k in sorted(range(1, n), key=lambda k: -min(k, n - k)):
            act(k)

    def remote(src, dst, send, recv, to):
        return pltpu.make_async_remote_copy(
            src_ref=src,
            dst_ref=dst,
            send_sem=send,
            recv_sem=recv,
            device_id=to,
            device_id_type=MESH,
        )

    def inner_copy(stage, k, src, dst, at=slice(None)):
        return remote(
            src.at[inner_peer(k), at],
            dst.at[inner, at],
            inner_send.at[stage, k],
            inner_recv.at[stage, k],
            inner_id(k),
        )

    def low_copy(stage, k, src, dst, half):
        return remote(
            src.at[half, low_peer(k)],
            dst.at[half, low],
            low_send.at[stage, k],
            low_recv.at[stage, k],
            low_id(k),
        )

    def high_copy(stage, k, src, dst, half):
        return remote(
            src.at[half],
            dst.at[half, high],
            high_send.at[stage, k],
            high_recv.at[stage, k],
            high_id(k),
        )

    def first_copy(half, k):
        return remote(
            send_first.at[half],
            firsts.at[half, low],
            low_send.at[9 + half, k],
            low_recv.at[9 + half, k],
            low_id(k),
        )

    def total_copy(k):
        return remote(
            send_total.at[inner_peer(k)],
            total1.at[inner],
            inner_send.at[0, k],
            inner_recv.at[0, k],
            inner_id(k),
        )

    def total2_copy(k):
        return remote(
            send_total2, total2.at[low], low_send.at[0, k], low_recv.at[0, k], low_id(k)
        )

    def total3_copy(k):
        return remote(
            send_total3, total3.at[high], high_send.at[0, k], high_recv.at[0, k], high_id(k)
        )

    def group_slices(group):
        return (
            pl.ds(pl.multiple_of(group * columns, columns), columns),
            pl.ds(pl.multiple_of(group * depth, depth), depth),
        )

    ORDER = sorted(range(1, n_inner), key=lambda k: -min(k, n_inner - k))

    def x_load(half, k):
        wide = group_slices(2 * inner_peer(k) + half)[0]
        return pltpu.make_async_copy(
            x_hbm.at[:, wide], x_ref.at[:, wide], load_sem.at[5 + half * n_inner + k]
        )

    def load(i, src, dst):
        return pltpu.make_async_copy(src, dst, load_sem.at[i])

    def init_load(half):
        rows = pl.ds(pl.multiple_of((half * ratio + low) * width, width), width)
        return load(half, init_hbm.at[rows], init_ref.at[half])

    load_in, load_grad, load_out = (
        load(2, in_hbm, in_ref),
        load(3, grad_hbm, grad_ref),
        load(4, out_hbm, out_ref),
    )
    load_in.start()
    for half in range(2):
        for k in ORDER + [0]:
            x_load(half, k).start()
    load_grad.start()
    load_out.start()
    init_load(0).start()
    init_load(1).start()

    barrier = pltpu.get_barrier_semaphore()
    for n, peer in ((n_inner, inner_id), (n_low, low_id), (n_high, high_id)):
        unrolled(
            n,
            lambda k, peer=peer: pl.semaphore_signal(
                barrier, inc=1, device_id=peer(k), device_id_type=MESH
            ),
        )

    def send_totals():
        totals = dot(decay_ref[...], jnp.ones((length, send_total.shape[2]), BF16), NN)
        for e in range(n_inner):
            send_total[e] = totals[e * 2 * ratio : (e + 1) * 2 * ratio]
        unrolled(n_inner, lambda k: total_copy(k).start())
        total1[inner] = send_total[inner]

    def half_rows(half):
        return pl.ds(half * columns, columns)

    def gain_of(half, k):
        group = 2 * inner_peer(k) + half
        wide, narrow = group_slices(group)
        x_load(half, k).wait()
        summed = spread_sums(decay_ref, group, ratio, width)
        from_start[:, wide] = jnp.exp(summed)
        factor = jnp.exp(summed[length - 1 :] - summed)
        to_end[:, wide] = factor
        weighted = (x_ref[:, wide].astype(F32) * factor).astype(BF16)
        weighted_ref[:, wide] = weighted
        return dot(weighted, in_ref[:, narrow], TN).astype(BF16)

    def own_of(half, k):
        wide, narrow = group_slices(2 * inner_peer(k) + half)
        scaled = (grad_ref[:, wide].astype(F32) * from_start[:, wide]).astype(BF16)
        scaled_ref[:, wide] = scaled
        return dot(scaled, out_ref[:, narrow], TN).astype(BF16)

    def local_part(group):
        wide, narrow = group_slices(group)
        picked = head_decays(decay_ref, group, ratio)
        below = lower(length)
        down = dot(below, picked, NT)
        across = dot(picked, below, NT)
        x, grad = x_ref[:, wide], grad_ref[:, wide]
        b, c = in_ref[:, narrow], out_ref[:, narrow]
        scores = dot(c, b, NT)
        causal = iota((length, length), 0) >= iota((length, length), 1)
        ys, dxs = [], []
        dscores = jnp.zeros((length, length), F32)
        for r in range(ratio):
            gap = down[:, r : r + 1] - across[r : r + 1, :]
            decays = jnp.exp(jnp.where(causal, gap, -1e30))
            weights = (scores * decays).astype(BF16)
            at = slice(r * width, (r + 1) * width)
            ys.append(dot(weights, x[:, at], NN))
            dxs.append(dot(weights, grad[:, at], TN))
            dscores = dscores + dot(grad[:, at], x[:, at], NT) * decays
        y_sum[:, wide] = jnp.concatenate(ys, axis=1)
        dx_sum[:, wide] = jnp.concatenate(dxs, axis=1)
        dscores = dscores.astype(BF16)
        dout_sum[:, narrow] = dot(dscores, b, NN)
        din_sum[:, narrow] = dot(dscores, c, TN)

    def place(group):
        heads = decay_ref.shape[0]
        head = group * ratio + iota((columns, heads), 0) // width
        return as_bf16(iota((columns, heads), 1) == head)

    def state_part(half, k):
        owner = around(inner, n_inner - k, n_inner)
        group = 2 * owner + half
        wide, narrow = group_slices(group)
        state = state_ref[owner, half_rows(half), :]
        y = y_sum[:, wide] + dot(out_ref[:, narrow], state, NT) * from_start[:, wide]
        y_ref[:, wide] = y.astype(BF16)
        dout = dout_sum[:, narrow] + dot(scaled_ref[:, wide], state, NN)
        dout_ref[:, narrow] = dout.astype(BF16)
        change = y * grad_ref[:, wide].astype(F32) - x_ref[:, wide].astype(F32) * dx_sum[:, wide]
        up_sum[...] += split_dot(change, place(group), NN)

    def part_stores(half, k):
        wide, narrow = group_slices(2 * around(inner, n_inner - k, n_inner) + half)
        return (
            store(4 + 2 * (half * n_inner + k), dx_ref.at[:, wide], dx_hbm.at[:, wide]),
            store(5 + 2 * (half * n_inner + k), din_ref.at[:, narrow], din_hbm.at[:, narrow]),
        )

    def after_part(half, k):
        owner = around(inner, n_inner - k, n_inner)
        group = 2 * owner + half
        wide, narrow = group_slices(group)
        state = state_ref[owner, half_rows(half), :]
        after = after_ref[owner, half_rows(half), :]
        far = dot(in_ref[:, narrow], after, NT) * to_end[:, wide]
        dx_ref[:, wide] = (dx_sum[:, wide] + far).astype(BF16)
        din = din_sum[:, narrow] + dot(weighted_ref[:, wide], after, NN)
        din_ref[:, narrow] = din.astype(BF16)
        low_sum[...] += split_dot(x_ref[:, wide].astype(F32) * far, place(group), NN)
        product = state.astype(F32) * after.astype(F32)
        picked = head_decays(decay_ref, group, ratio)
        total = dot(picked, jnp.ones((length, depth), BF16), NN)
        state_sum[pl.ds(pl.multiple_of(group * ratio, ratio), ratio), :] = jnp.sum(
            product.reshape(ratio, width, depth), axis=1
        ) * jnp.exp(total)
        for copy in part_stores(half, k):
            copy.start()

    def local_parts(start, stop):
        def body(group, none):
            local_part(group)
            return none

        groups = n_inner * 2
        lax.fori_loop(start * groups // 8, stop * groups // 8, body, 0)

    def parts(stage, half, part):
        part(half, 0)
        for k in ORDER:
            inner_copy(stage[0] + half, k, stage[1], stage[2], half_rows(half)).wait_recv()
            part(half, k)

    def store(i, src, dst):
        return pltpu.make_async_copy(src, dst, store_sem.at[i])

    def fill_gain(half, k):
        send_gain[inner_peer(k), half_rows(half), :] = gain_of(half, k)

    def send_gains(half, start):
        for k in ORDER[start:]:
            fill_gain(half, k)
            inner_copy(1 + half, k, send_gain, gain1, half_rows(half)).start()
        gain1[inner, half_rows(half), :] = gain_of(half, 0)

    def fill_owns(half):
        at = half_rows(half)

        def act(k):
            send_own[inner_peer(k), at, :] = own_of(half, k)

        each(n_inner, act)
        own1[inner, at, :] = own_of(half, 0)

    def send_inner(stage, src, dst, half):
        for k in ORDER:
            inner_copy(stage + half, k, src, dst, half_rows(half)).start()

    def recv_inner(stage, src, dst, half):
        unrolled(n_inner, lambda k: inner_copy(stage + half, k, src, dst, half_rows(half)).wait_recv())

    def sent_inner(stage, src, dst, half):
        unrolled(n_inner, lambda k: inner_copy(stage + half, k, src, dst, half_rows(half)).wait_send())

    def keep_inner(src, dst, half):
        at = half_rows(half)
        dst[inner, at, :] = src[inner, at, :]

    def send_low(stage, src, dst, half):
        unrolled(n_low, lambda k: low_copy(stage + half, k, src, dst, half).start())
        dst[half, low] = src[half, low]

    def recv_low(stage, src, dst, half):
        unrolled(n_low, lambda k: low_copy(stage + half, k, src, dst, half).wait_recv())

    def sent_low(stage, src, dst, half):
        unrolled(n_low, lambda k: low_copy(stage + half, k, src, dst, half).wait_send())

    def send_high(stage, src, dst, half):
        unrolled(n_high, lambda k: high_copy(stage + half, k, src, dst, half).start())
        dst[half, high] = src[half]

    def recv_high(stage, src, dst, half):
        unrolled(n_high, lambda k: high_copy(stage + half, k, src, dst, half).wait_recv())

    def sent_high(stage, src, dst, half):
        unrolled(n_high, lambda k: high_copy(stage + half, k, src, dst, half).wait_send())

    def factor1(e, head):
        return jnp.exp(total1[e, pl.ds(head, 1), :])

    def factor2(e, half):
        return jnp.exp(total2[e, pl.ds(half * ratio + low, 1), :])

    def factor3(e, half):
        return jnp.exp(total3[e, pl.ds(half * ratio + low, 1), :])

    def head_rows(head):
        return pl.ds(pl.multiple_of(head * width, width), width)

    def fold_gains(half):
        def body(r, none):
            head = half * ratio + r
            at = head_rows(head)
            value = gain1[0, at, :].astype(F32)
            for e in range(1, n_inner):
                value = factor1(e, head) * value + gain1[e, at, :].astype(F32)
            send_gain2[half, r] = value.astype(BF16)
            return none

        lax.fori_loop(0, ratio, body, 0, unroll=4)

    def fold_owns(half):
        def body(r, none):
            head = half * ratio + r
            at = head_rows(head)
            value = own1[n_inner - 1, at, :].astype(F32)
            for e in range(n_inner - 2, -1, -1):
                value = factor1(e, head) * value + own1[e, at, :].astype(F32)
            send_own2[half, r] = value.astype(BF16)
            return none

        lax.fori_loop(0, ratio, body, 0, unroll=4)

    def fold_gains2(half):
        value = gain2[half, 0].astype(F32)
        for e in range(1, n_low):
            value = factor2(e, half) * value + gain2[half, e].astype(F32)
        send_gain3[half] = value.astype(BF16)

    def fold_owns2(half):
        value = own2[half, n_low - 1].astype(F32)
        for e in range(n_low - 2, -1, -1):
            value = factor2(e, half) * value + own2[half, e].astype(F32)
        send_own3[half] = value.astype(BF16)

    def spread_states(half):
        value = init_ref[half]
        for e in range(n_high - 1):
            later = factor3(e, half) * value + gain3[half, e].astype(F32)
            value = jnp.where(e < high, later, value)
        for e in range(n_low):
            send_before[half, e] = value.astype(BF16)
            if e < n_low - 1:
                value = factor2(e, half) * value + gain2[half, e].astype(F32)

    def spread_afters(half):
        value = jnp.zeros(init_ref.shape[1:], F32)
        first = value
        for e in range(n_high - 1, -1, -1):
            first = factor3(e, half) * first + own3[half, e].astype(F32)
            value = jnp.where(e > high, first, value)
        send_first[half] = first.astype(BF16)
        for e in range(n_low - 1, -1, -1):
            send_behind[half, e] = value.astype(BF16)
            if e > 0:
                value = factor2(e, half) * value + own2[half, e].astype(F32)

    def fill_states(half):
        def body(r, none):
            head = half * ratio + r
            at = head_rows(head)
            value = before[half, r].astype(F32)
            for e in range(n_inner):
                send_state[e, at, :] = value.astype(BF16)
                if e < n_inner - 1:
                    value = factor1(e, head) * value + gain1[e, at, :].astype(F32)
            return none

        lax.fori_loop(0, ratio, body, 0, unroll=4)
        keep_inner(send_state, state_ref, half)

    def fill_afters(half):
        def body(r, none):
            head = half * ratio + r
            at = head_rows(head)
            value = behind[half, r].astype(F32)
            for e in range(n_inner - 1, -1, -1):
                send_after[e, at, :] = value.astype(BF16)
                if e > 0:
                    value = factor1(e, head) * value + own1[e, at, :].astype(F32)
            return none

        lax.fori_loop(0, ratio, body, 0, unroll=4)
        keep_inner(send_after, after_ref, half)

    def send_firsts(half):
        unrolled(n_low, lambda k: first_copy(half, k).start())
        firsts[half, low] = send_first[half]

    def put_firsts(half):
        unrolled(n_low, lambda k: first_copy(half, k).wait_recv())
        for r in range(ratio):
            start_ref[pl.ds((half * ratio + r) * width, width), :] = firsts[half, r].astype(F32)

    gains, owns = (1, send_gain, gain1), (3, send_own, own1)
    states, afters = (5, send_state, state_ref), (7, send_after, after_ref)
    gains2, owns2 = (1, send_gain2, gain2), (3, send_own2, own2)
    befores, behinds = (5, send_before, before), (7, send_behind, behind)
    gains3, owns3 = (1, send_gain3, gain3), (3, send_own3, own3)

    up_sum[...] = jnp.zeros_like(up_sum)
    low_sum[...] = jnp.zeros_like(low_sum)
    load_in.wait()
    fill_gain(0, ORDER[0])
    pl.semaphore_wait(barrier, n_inner + n_low + n_high - 3)
    send_totals()
    inner_copy(1, ORDER[0], send_gain, gain1, half_rows(0)).start()
    send_gains(0, 1)
    send_gains(1, 0)
    load_grad.wait()
    load_out.wait()
    fill_owns(0)

    unrolled(n_inner, lambda k: total_copy(k).wait_recv())
    row = total1[0]
    for e in range(1, n_inner):
        row = row + total1[e]
    send_total2[...] = row
    total2[low] = row
    unrolled(n_low, lambda k: total2_copy(k).start())
    fill_owns(1)
    local_parts(0, 2)

    unrolled(n_low, lambda k: total2_copy(k).wait_recv())
    row = total2[0]
    for e in range(1, n_low):
        row = row + total2[e]
    send_total3[...] = row
    total3[high] = row
    unrolled(n_high, lambda k: total3_copy(k).start())
    recv_inner(*gains, 0)
    fold_gains(0)
    send_low(*gains2, 0)
    send_inner(*owns, 0)
    local_parts(2, 6)
    recv_low(*gains2, 0)
    fold_gains2(0)
    send_high(*gains3, 0)
    recv_inner(*gains, 1)
    fold_gains(1)
    send_low(*gains2, 1)
    send_inner(*owns, 1)
    local_parts(6, 8)
    init_load(0).wait()
    init_load(1).wait()
    unrolled(n_high, lambda k: total3_copy(k).wait_recv())
    recv_high(*gains3, 0)
    spread_states(0)
    send_low(*befores, 0)
    recv_low(*gains2, 1)
    fold_gains2(1)
    send_high(*gains3, 1)
    recv_inner(*owns, 0)
    fold_owns(0)
    send_low(*owns2, 0)
    recv_low(*befores, 0)
    fill_states(0)
    send_inner(*states, 0)
    recv_high(*gains3, 1)
    spread_states(1)
    send_low(*befores, 1)
    recv_low(*owns2, 0)
    fold_owns2(0)
    send_high(*owns3, 0)
    recv_inner(*owns, 1)
    fold_owns(1)
    send_low(*owns2, 1)
    recv_low(*befores, 1)
    fill_states(1)
    send_inner(*states, 1)
    recv_high(*owns3, 0)
    spread_afters(0)
    send_low(*behinds, 0)
    send_firsts(0)
    recv_low(*owns2, 1)
    fold_owns2(1)
    send_high(*owns3, 1)
    parts(states, 0, state_part)
    recv_low(*behinds, 0)
    fill_afters(0)
    send_inner(*afters, 0)
    recv_high(*owns3, 1)
    spread_afters(1)
    send_low(*behinds, 1)
    send_firsts(1)
    parts(states, 1, state_part)
    recv_low(*behinds, 1)
    fill_afters(1)
    send_inner(*afters, 1)
    put_firsts(0)
    put_firsts(1)
    for half in range(2):
        unrolled(n_low, lambda k, half=half: first_copy(half, k).wait_send())
    store_start = store(0, start_ref, dstart_hbm)
    store_start.start()
    stores = [store(1, y_ref, y_hbm), store(2, dout_ref, dout_hbm)]
    for copy in stores:
        copy.start()

    unrolled(n_inner, lambda k: total_copy(k).wait_send())
    unrolled(n_low, lambda k: total2_copy(k).wait_send())
    unrolled(n_high, lambda k: total3_copy(k).wait_send())
    for half in range(2):
        for stage in (gains2, owns2, befores, behinds):
            sent_low(*stage, half)
        for stage in (gains3, owns3):
            sent_high(*stage, half)
        for stage in (gains, owns, states):
            sent_inner(*stage, half)
    row = iota((length, length), 0)
    column = iota((length, length), 1)
    up_total = exact_dot(up_sum[...], jnp.where(row >= column, 1.0, 0.0), TN)
    parts(afters, 0, after_part)
    parts(afters, 1, after_part)
    sent_inner(*afters, 0)
    sent_inner(*afters, 1)

    ddecay_ref[...] = (
        up_total
        + exact_dot(low_sum[...], jnp.where(row < column, 1.0, 0.0), TN)
        + jnp.sum(state_sum[...], axis=1, keepdims=True)
    ).astype(BF16)
    end = store(3, ddecay_ref, ddecay_hbm)
    end.start()
    for copy in [store_start] + stores + [end]:
        copy.wait()
    for half in range(2):
        for k in range(n_inner):
            for copy in part_stores(half, k):
                copy.wait()


def carry(x, decay, read_in, read_out, grad, init, n_outer, n_inner, width, depth):
    length = x.shape[0]
    groups = read_in.shape[1] // depth
    heads = decay.shape[0]
    ratio = heads // groups
    mine = heads // n_inner
    n_low = ratio
    n_high = n_outer // n_low
    vmem = pl.BlockSpec(memory_space=pltpu.VMEM)
    hbm = pl.BlockSpec(memory_space=pl.ANY)
    chunks = pltpu.VMEM((n_inner, mine * width, depth), BF16)
    runs = pltpu.VMEM((2, n_low, width, depth), BF16)
    head = pltpu.VMEM((2, width, depth), BF16)
    highs = pltpu.VMEM((2, n_high, width, depth), BF16)
    total = pltpu.VMEM((mine, depth), F32)
    wide = jax.ShapeDtypeStruct(x.shape, BF16)
    narrow = jax.ShapeDtypeStruct(read_in.shape, BF16)
    wide32 = pltpu.VMEM(x.shape, F32)
    narrow32 = pltpu.VMEM(read_in.shape, F32)
    dma = pltpu.SemaphoreType.DMA
    return pl.pallas_call(
        functools.partial(carry_kernel, n_inner, n_low, n_high, ratio, width),
        in_specs=[hbm, vmem, hbm, hbm, hbm, hbm],
        out_specs=[hbm] * 6,
        out_shape=[
            wide,
            wide,
            jax.ShapeDtypeStruct(decay.shape, BF16),
            narrow,
            narrow,
            jax.ShapeDtypeStruct((mine * width, depth), F32),
        ],
        scratch_shapes=[
            chunks,
            chunks,
            pltpu.VMEM((mine * width, depth), F32),
            wide32,
            wide32,
            pltpu.VMEM(x.shape, BF16),
            pltpu.VMEM(x.shape, BF16),
            wide32,
            wide32,
            narrow32,
            narrow32,
            pltpu.VMEM((length, heads), F32),
            pltpu.VMEM((length, heads), F32),
            pltpu.VMEM((heads, depth), F32),
            pltpu.VMEM(x.shape, BF16),
            pltpu.VMEM(x.shape, BF16),
            pltpu.VMEM(decay.shape, BF16),
            pltpu.VMEM(read_in.shape, BF16),
            pltpu.VMEM(read_out.shape, BF16),
            pltpu.VMEM(x.shape, BF16),
            pltpu.VMEM(read_in.shape, BF16),
            pltpu.VMEM(read_out.shape, BF16),
            pltpu.VMEM(grad.shape, BF16),
            pltpu.VMEM((2, width, depth), F32),
            pltpu.VMEM((n_inner, mine, depth), F32),
            pltpu.VMEM((n_inner, mine, depth), F32),
            total,
            pltpu.VMEM((n_low, mine, depth), F32),
            total,
            pltpu.VMEM((n_high, mine, depth), F32),
            chunks,
            chunks,
            chunks,
            chunks,
            runs,
            runs,
            runs,
            runs,
            head,
            highs,
            head,
            highs,
            runs,
            runs,
            runs,
            runs,
            head,
            runs,
            chunks,
            chunks,
            dma((5 + 2 * n_inner,)),
            dma((4 + 4 * n_inner,)),
            dma((9, n_inner)),
            dma((9, n_inner)),
            dma((11, n_low)),
            dma((11, n_low)),
            dma((5, n_high)),
            dma((5, n_high)),
            pltpu.SemaphoreType.REGULAR((2,)),
        ],
        compiler_params=pltpu.CompilerParams(
            collective_id=0, has_side_effects=True, vmem_limit_bytes=60 * 2**20
        ),
        name="carry",
    )(x, decay, read_in, read_out, grad, init)


def deliver_kernel(parts, *refs):
    n = len(parts)
    hbm, out, held, (loaded, stored) = refs[:n], refs[n : 2 * n], refs[2 * n : 3 * n], refs[3 * n :]
    loads, stores = [], []
    for i, part in enumerate(parts):
        rows = hbm[i].shape[0] // part
        for p in range(part):
            at, sem = pl.ds(p * rows, rows), len(loads)
            loads.append(
                pltpu.make_async_copy(hbm[i].at[at], held[i].at[at], loaded.at[sem])
            )
            stores.append(
                pltpu.make_async_copy(held[i].at[at], out[i].at[at], stored.at[sem])
            )
    for load in loads:
        load.start()
    for load, store in zip(loads, stores):
        load.wait()
        store.start()
    for store in stores:
        store.wait()


def deliver(*arrays):
    n = len(arrays)
    hbm = pl.BlockSpec(memory_space=pl.ANY)
    parts = [4 if a.size >= 2**19 else 1 for a in arrays]
    return pl.pallas_call(
        functools.partial(deliver_kernel, parts),
        in_specs=[hbm] * n,
        out_specs=[hbm] * n,
        out_shape=[jax.ShapeDtypeStruct(a.shape, a.dtype) for a in arrays],
        scratch_shapes=[pltpu.VMEM(a.shape, a.dtype) for a in arrays]
        + [pltpu.SemaphoreType.DMA((sum(parts),))] * 2,
        compiler_params=pltpu.CompilerParams(vmem_limit_bytes=60 * 2**20),
        name="deliver",
    )(*arrays)


def shards(inputs, log_decay, read_in, read_out, initial_state, output_grad):
    n_outer, n_inner = lax.axis_size("outer"), lax.axis_size("inner")
    width, depth = initial_state.shape[1:]
    decay = log_decay.T
    results = carry(
        inputs,
        decay,
        read_in,
        read_out,
        output_grad,
        initial_state.reshape(-1, depth),
        n_outer,
        n_inner,
        width,
        depth,
    )
    y, dx, ddecay, din, dout, dstart = deliver(*results)
    return (y, dx, ddecay.T, din, dout, dstart.reshape(initial_state.shape))


def solution(mesh):
    tokens = P(("outer", "inner"), None)
    held = P("inner", None, None)
    return jax.shard_map(
        shards,
        mesh=mesh,
        in_specs=(tokens, tokens, tokens, tokens, held, tokens),
        out_specs=(tokens, tokens, tokens, tokens, tokens, held),
        check_vma=False,
    )
```

```python
import functools

import jax
import jax.numpy as jnp
from jax import lax
from jax.experimental import pallas as pl
from jax.experimental.pallas import tpu as pltpu
from jax.sharding import PartitionSpec as P

F32 = jnp.float32
BF16 = jnp.bfloat16
NN = ((1,), (0,))
NT = ((1,), (1,))
TN = ((0,), (0,))
MESH = pl.DeviceIdType.MESH


def dot(a, b, dims):
    return lax.dot_general(a, b, (dims, ((), ())), preferred_element_type=F32)


def exact_dot(a, b, dims):
    return lax.dot_general(
        a, b, (dims, ((), ())), preferred_element_type=F32, precision=lax.Precision.HIGHEST
    )


def split_dot(a, b, dims):
    high = a.astype(BF16)
    low = (a - high.astype(F32)).astype(BF16)
    return dot(high, b, dims) + dot(low, b, dims)


def iota(shape, axis):
    return lax.broadcasted_iota(jnp.int32, shape, axis)


def as_bf16(mask):
    return jnp.where(mask, 1.0, 0.0).astype(BF16)


def lower(length):
    return as_bf16(iota((length, length), 0) >= iota((length, length), 1))


def spread_sums(decay_ref, group, ratio, width):
    heads, length = decay_ref.shape
    columns = ratio * width
    pick = as_bf16(iota((heads, columns), 0) == group * ratio + iota((heads, columns), 1) // width)
    return dot(lower(length), dot(decay_ref[...], pick, TN).astype(BF16), NN)


def head_decays(decay_ref, group, ratio):
    heads, length = decay_ref.shape
    pick = as_bf16(iota((ratio, heads), 1) == group * ratio + iota((ratio, heads), 0))
    return dot(pick, decay_ref[...], NN).astype(BF16)


def carry_kernel(
    n_inner,
    n_low,
    n_high,
    ratio,
    width,
    x_hbm,
    decay_ref,
    in_hbm,
    out_hbm,
    grad_hbm,
    init_hbm,
    y_hbm,
    dx_hbm,
    ddecay_hbm,
    din_hbm,
    dout_hbm,
    dstart_hbm,
    state_ref,
    after_ref,
    start_ref,
    from_start,
    to_end,
    weighted_ref,
    scaled_ref,
    y_sum,
    dx_sum,
    din_sum,
    dout_sum,
    up_sum,
    low_sum,
    state_sum,
    y_ref,
    dx_ref,
    ddecay_ref,
    din_ref,
    dout_ref,
    x_ref,
    in_ref,
    out_ref,
    grad_ref,
    init_ref,
    send_total,
    total1,
    send_total2,
    total2,
    send_total3,
    total3,
    send_gain,
    gain1,
    send_own,
    own1,
    send_gain2,
    gain2,
    send_own2,
    own2,
    send_gain3,
    gain3,
    send_own3,
    own3,
    send_before,
    before,
    send_behind,
    behind,
    send_first,
    firsts,
    send_state,
    send_after,
    load_sem,
    store_sem,
    inner_send,
    inner_recv,
    low_send,
    low_recv,
    high_send,
    high_recv,
    ready,
):
    outer = lax.axis_index("outer")
    inner = lax.axis_index("inner")
    low = lax.rem(outer, n_low)
    high = lax.div(outer, n_low)
    length = x_ref.shape[0]
    depth = in_ref.shape[1] * ratio // decay_ref.shape[0]
    columns = ratio * width

    def around(here, k, n):
        there = here + k
        return jnp.where(there >= n, there - n, there)

    def inner_peer(k):
        return around(inner, k, n_inner)

    def low_peer(k):
        return around(low, k, n_low)

    def high_peer(k):
        return around(high, k, n_high)

    def inner_id(k):
        return (outer, inner_peer(k))

    def low_id(k):
        return (high * n_low + low_peer(k), inner)

    def high_id(k):
        return (high_peer(k) * n_low + low, inner)

    def each(n, act):
        def body(k, none):
            act(k)
            return none

        lax.fori_loop(1, n, body, 0)

    def unrolled(n, act):
        for k in sorted(range(1, n), key=lambda k: -min(k, n - k)):
            act(k)

    def remote(src, dst, send, recv, to):
        return pltpu.make_async_remote_copy(
            src_ref=src,
            dst_ref=dst,
            send_sem=send,
            recv_sem=recv,
            device_id=to,
            device_id_type=MESH,
        )

    def inner_copy(stage, k, src, dst, at=slice(None)):
        return remote(
            src.at[inner_peer(k), at],
            dst.at[inner, at],
            inner_send.at[stage, k],
            inner_recv.at[stage, k],
            inner_id(k),
        )

    def low_copy(stage, k, src, dst, half):
        return remote(
            src.at[half, low_peer(k)],
            dst.at[half, low],
            low_send.at[stage, k],
            low_recv.at[stage, k],
            low_id(k),
        )

    def high_copy(stage, k, src, dst, half):
        return remote(
            src.at[half],
            dst.at[half, high],
            high_send.at[stage, k],
            high_recv.at[stage, k],
            high_id(k),
        )

    def first_copy(half, k):
        return remote(
            send_first.at[half],
            firsts.at[half, low],
            low_send.at[9 + half, k],
            low_recv.at[9 + half, k],
            low_id(k),
        )

    def total_copy(k):
        return remote(
            send_total.at[inner_peer(k)],
            total1.at[inner],
            inner_send.at[0, k],
            inner_recv.at[0, k],
            inner_id(k),
        )

    def total2_copy(k):
        return remote(
            send_total2, total2.at[low], low_send.at[0, k], low_recv.at[0, k], low_id(k)
        )

    def total3_copy(k):
        return remote(
            send_total3, total3.at[high], high_send.at[0, k], high_recv.at[0, k], high_id(k)
        )

    def group_slices(group):
        return (
            pl.ds(pl.multiple_of(group * columns, columns), columns),
            pl.ds(pl.multiple_of(group * depth, depth), depth),
        )

    ORDER = sorted(range(1, n_inner), key=lambda k: -min(k, n_inner - k))

    def x_load(half, k):
        wide = group_slices(2 * inner_peer(k) + half)[0]
        return pltpu.make_async_copy(
            x_hbm.at[:, wide], x_ref.at[:, wide], load_sem.at[5 + half * n_inner + k]
        )

    def load(i, src, dst):
        return pltpu.make_async_copy(src, dst, load_sem.at[i])

    def init_load(half):
        rows = pl.ds(pl.multiple_of((half * ratio + low) * width, width), width)
        return load(half, init_hbm.at[rows], init_ref.at[half])

    load_in, load_grad, load_out = (
        load(2, in_hbm, in_ref),
        load(3, grad_hbm, grad_ref),
        load(4, out_hbm, out_ref),
    )
    load_in.start()
    for half in range(2):
        for k in ORDER + [0]:
            x_load(half, k).start()
    load_grad.start()
    load_out.start()
    init_load(0).start()
    init_load(1).start()

    barrier = pltpu.get_barrier_semaphore()
    for n, peer in ((n_inner, inner_id), (n_low, low_id), (n_high, high_id)):
        unrolled(
            n,
            lambda k, peer=peer: pl.semaphore_signal(
                barrier, inc=1, device_id=peer(k), device_id_type=MESH
            ),
        )

    def send_totals():
        totals = dot(decay_ref[...], jnp.ones((length, send_total.shape[2]), BF16), NN)
        for e in range(n_inner):
            send_total[e] = totals[e * 2 * ratio : (e + 1) * 2 * ratio]
        unrolled(n_inner, lambda k: total_copy(k).start())
        total1[inner] = send_total[inner]

    def half_rows(half):
        return pl.ds(half * columns, columns)

    def gain_of(half, k):
        group = 2 * inner_peer(k) + half
        wide, narrow = group_slices(group)
        x_load(half, k).wait()
        summed = spread_sums(decay_ref, group, ratio, width)
        from_start[:, wide] = jnp.exp(summed)
        factor = jnp.exp(summed[length - 1 :] - summed)
        to_end[:, wide] = factor
        weighted = (x_ref[:, wide].astype(F32) * factor).astype(BF16)
        weighted_ref[:, wide] = weighted
        return dot(weighted, in_ref[:, narrow], TN).astype(BF16)

    def own_of(half, k):
        wide, narrow = group_slices(2 * inner_peer(k) + half)
        scaled = (grad_ref[:, wide].astype(F32) * from_start[:, wide]).astype(BF16)
        scaled_ref[:, wide] = scaled
        return dot(scaled, out_ref[:, narrow], TN).astype(BF16)

    def local_part(group):
        wide, narrow = group_slices(group)
        picked = head_decays(decay_ref, group, ratio)
        below = lower(length)
        down = dot(below, picked, NT)
        across = dot(picked, below, NT)
        x, grad = x_ref[:, wide], grad_ref[:, wide]
        b, c = in_ref[:, narrow], out_ref[:, narrow]
        scores = dot(c, b, NT)
        causal = iota((length, length), 0) >= iota((length, length), 1)
        ys, dxs = [], []
        dscores = jnp.zeros((length, length), F32)
        for r in range(ratio):
            gap = down[:, r : r + 1] - across[r : r + 1, :]
            decays = jnp.exp(jnp.where(causal, gap, -1e30))
            weights = (scores * decays).astype(BF16)
            at = slice(r * width, (r + 1) * width)
            ys.append(dot(weights, x[:, at], NN))
            dxs.append(dot(weights, grad[:, at], TN))
            dscores = dscores + dot(grad[:, at], x[:, at], NT) * decays
        y_sum[:, wide] = jnp.concatenate(ys, axis=1)
        dx_sum[:, wide] = jnp.concatenate(dxs, axis=1)
        dscores = dscores.astype(BF16)
        dout_sum[:, narrow] = dot(dscores, b, NN)
        din_sum[:, narrow] = dot(dscores, c, TN)

    def place(group):
        heads = decay_ref.shape[0]
        head = group * ratio + iota((columns, heads), 0) // width
        return as_bf16(iota((columns, heads), 1) == head)

    def state_part(half, k):
        owner = around(inner, n_inner - k, n_inner)
        group = 2 * owner + half
        wide, narrow = group_slices(group)
        state = state_ref[owner, half_rows(half), :]
        y = y_sum[:, wide] + dot(out_ref[:, narrow], state, NT) * from_start[:, wide]
        y_ref[:, wide] = y.astype(BF16)
        dout = dout_sum[:, narrow] + dot(scaled_ref[:, wide], state, NN)
        dout_ref[:, narrow] = dout.astype(BF16)
        change = y * grad_ref[:, wide].astype(F32) - x_ref[:, wide].astype(F32) * dx_sum[:, wide]
        up_sum[...] += split_dot(change, place(group), NN)

    def part_stores(half, k):
        wide, narrow = group_slices(2 * around(inner, n_inner - k, n_inner) + half)
        return (
            store(4 + 2 * (half * n_inner + k), dx_ref.at[:, wide], dx_hbm.at[:, wide]),
            store(5 + 2 * (half * n_inner + k), din_ref.at[:, narrow], din_hbm.at[:, narrow]),
        )

    def after_part(half, k):
        owner = around(inner, n_inner - k, n_inner)
        group = 2 * owner + half
        wide, narrow = group_slices(group)
        state = state_ref[owner, half_rows(half), :]
        after = after_ref[owner, half_rows(half), :]
        far = dot(in_ref[:, narrow], after, NT) * to_end[:, wide]
        dx_ref[:, wide] = (dx_sum[:, wide] + far).astype(BF16)
        din = din_sum[:, narrow] + dot(weighted_ref[:, wide], after, NN)
        din_ref[:, narrow] = din.astype(BF16)
        low_sum[...] += split_dot(x_ref[:, wide].astype(F32) * far, place(group), NN)
        product = state.astype(F32) * after.astype(F32)
        picked = head_decays(decay_ref, group, ratio)
        total = dot(picked, jnp.ones((length, depth), BF16), NN)
        state_sum[pl.ds(pl.multiple_of(group * ratio, ratio), ratio), :] = jnp.sum(
            product.reshape(ratio, width, depth), axis=1
        ) * jnp.exp(total)
        for copy in part_stores(half, k):
            copy.start()

    def local_parts(start, stop):
        def body(group, none):
            local_part(group)
            return none

        groups = n_inner * 2
        lax.fori_loop(start * groups // 8, stop * groups // 8, body, 0)

    def parts(stage, half, part):
        part(half, 0)
        for k in ORDER:
            inner_copy(stage[0] + half, k, stage[1], stage[2], half_rows(half)).wait_recv()
            part(half, k)

    def store(i, src, dst):
        return pltpu.make_async_copy(src, dst, store_sem.at[i])

    def fill_gain(half, k):
        send_gain[inner_peer(k), half_rows(half), :] = gain_of(half, k)

    def send_gains(half, start):
        for k in ORDER[start:]:
            fill_gain(half, k)
            inner_copy(1 + half, k, send_gain, gain1, half_rows(half)).start()
        gain1[inner, half_rows(half), :] = gain_of(half, 0)

    def fill_owns(half):
        at = half_rows(half)

        def act(k):
            send_own[inner_peer(k), at, :] = own_of(half, k)

        each(n_inner, act)
        own1[inner, at, :] = own_of(half, 0)

    def send_inner(stage, src, dst, half):
        for k in ORDER:
            inner_copy(stage + half, k, src, dst, half_rows(half)).start()

    def recv_inner(stage, src, dst, half):
        unrolled(n_inner, lambda k: inner_copy(stage + half, k, src, dst, half_rows(half)).wait_recv())

    def sent_inner(stage, src, dst, half):
        unrolled(n_inner, lambda k: inner_copy(stage + half, k, src, dst, half_rows(half)).wait_send())

    def keep_inner(src, dst, half):
        at = half_rows(half)
        dst[inner, at, :] = src[inner, at, :]

    def send_low(stage, src, dst, half):
        unrolled(n_low, lambda k: low_copy(stage + half, k, src, dst, half).start())
        dst[half, low] = src[half, low]

    def recv_low(stage, src, dst, half):
        unrolled(n_low, lambda k: low_copy(stage + half, k, src, dst, half).wait_recv())

    def sent_low(stage, src, dst, half):
        unrolled(n_low, lambda k: low_copy(stage + half, k, src, dst, half).wait_send())

    def send_high(stage, src, dst, half):
        unrolled(n_high, lambda k: high_copy(stage + half, k, src, dst, half).start())
        dst[half, high] = src[half]

    def recv_high(stage, src, dst, half):
        unrolled(n_high, lambda k: high_copy(stage + half, k, src, dst, half).wait_recv())

    def sent_high(stage, src, dst, half):
        unrolled(n_high, lambda k: high_copy(stage + half, k, src, dst, half).wait_send())

    def factor1(e, head):
        return jnp.exp(total1[e, pl.ds(head, 1), :])

    def factor2(e, half):
        return jnp.exp(total2[e, pl.ds(half * ratio + low, 1), :])

    def factor3(e, half):
        return jnp.exp(total3[e, pl.ds(half * ratio + low, 1), :])

    def head_rows(head):
        return pl.ds(pl.multiple_of(head * width, width), width)

    def fold_gains(half):
        def fold(r):
            head = half * ratio + r
            at = head_rows(head)
            value = gain1[0, at, :].astype(F32)
            for e in range(1, n_inner):
                value = factor1(e, head) * value + gain1[e, at, :].astype(F32)
            return value.astype(BF16)

        def act(k):
            send_gain2[half, low_peer(k)] = fold(low_peer(k))
            low_copy(1 + half, k, send_gain2, gain2, half).start()

        unrolled(n_low, act)
        gain2[half, low] = fold(low)

    def fold_owns(half):
        def fold(r):
            head = half * ratio + r
            at = head_rows(head)
            value = own1[n_inner - 1, at, :].astype(F32)
            for e in range(n_inner - 2, -1, -1):
                value = factor1(e, head) * value + own1[e, at, :].astype(F32)
            return value.astype(BF16)

        def act(k):
            send_own2[half, low_peer(k)] = fold(low_peer(k))
            low_copy(3 + half, k, send_own2, own2, half).start()

        unrolled(n_low, act)
        own2[half, low] = fold(low)

    def fold_gains2(half):
        value = gain2[half, 0].astype(F32)
        for e in range(1, n_low):
            value = factor2(e, half) * value + gain2[half, e].astype(F32)
        send_gain3[half] = value.astype(BF16)

    def fold_owns2(half):
        value = own2[half, n_low - 1].astype(F32)
        for e in range(n_low - 2, -1, -1):
            value = factor2(e, half) * value + own2[half, e].astype(F32)
        send_own3[half] = value.astype(BF16)

    def spread_states(half):
        value = init_ref[half]
        for e in range(n_high - 1):
            later = factor3(e, half) * value + gain3[half, e].astype(F32)
            value = jnp.where(e < high, later, value)
        for e in range(n_low):
            send_before[half, e] = value.astype(BF16)
            if e < n_low - 1:
                value = factor2(e, half) * value + gain2[half, e].astype(F32)

    def spread_afters(half):
        value = jnp.zeros(init_ref.shape[1:], F32)
        first = value
        for e in range(n_high - 1, -1, -1):
            first = factor3(e, half) * first + own3[half, e].astype(F32)
            value = jnp.where(e > high, first, value)
        send_first[half] = first.astype(BF16)
        for e in range(n_low - 1, -1, -1):
            send_behind[half, e] = value.astype(BF16)
            if e > 0:
                value = factor2(e, half) * value + own2[half, e].astype(F32)

    def fill_states(half):
        def body(r, none):
            head = half * ratio + r
            at = head_rows(head)
            value = before[half, r].astype(F32)
            for e in range(n_inner):
                send_state[e, at, :] = value.astype(BF16)
                if e < n_inner - 1:
                    value = factor1(e, head) * value + gain1[e, at, :].astype(F32)
            return none

        lax.fori_loop(0, ratio, body, 0, unroll=4)
        keep_inner(send_state, state_ref, half)

    def fill_afters(half):
        def body(r, none):
            head = half * ratio + r
            at = head_rows(head)
            value = behind[half, r].astype(F32)
            for e in range(n_inner - 1, -1, -1):
                send_after[e, at, :] = value.astype(BF16)
                if e > 0:
                    value = factor1(e, head) * value + own1[e, at, :].astype(F32)
            return none

        lax.fori_loop(0, ratio, body, 0, unroll=4)
        keep_inner(send_after, after_ref, half)

    def send_firsts(half):
        unrolled(n_low, lambda k: first_copy(half, k).start())
        firsts[half, low] = send_first[half]

    def put_firsts(half):
        unrolled(n_low, lambda k: first_copy(half, k).wait_recv())
        for r in range(ratio):
            start_ref[pl.ds((half * ratio + r) * width, width), :] = firsts[half, r].astype(F32)

    gains, owns = (1, send_gain, gain1), (3, send_own, own1)
    states, afters = (5, send_state, state_ref), (7, send_after, after_ref)
    gains2, owns2 = (1, send_gain2, gain2), (3, send_own2, own2)
    befores, behinds = (5, send_before, before), (7, send_behind, behind)
    gains3, owns3 = (1, send_gain3, gain3), (3, send_own3, own3)

    up_sum[...] = jnp.zeros_like(up_sum)
    low_sum[...] = jnp.zeros_like(low_sum)
    load_in.wait()
    fill_gain(0, ORDER[0])
    pl.semaphore_wait(barrier, n_inner + n_low + n_high - 3)
    send_totals()
    inner_copy(1, ORDER[0], send_gain, gain1, half_rows(0)).start()
    send_gains(0, 1)
    send_gains(1, 0)
    load_grad.wait()
    load_out.wait()
    fill_owns(0)

    unrolled(n_inner, lambda k: total_copy(k).wait_recv())
    row = total1[0]
    for e in range(1, n_inner):
        row = row + total1[e]
    send_total2[...] = row
    total2[low] = row
    unrolled(n_low, lambda k: total2_copy(k).start())
    fill_owns(1)
    local_parts(0, 2)

    unrolled(n_low, lambda k: total2_copy(k).wait_recv())
    row = total2[0]
    for e in range(1, n_low):
        row = row + total2[e]
    send_total3[...] = row
    total3[high] = row
    unrolled(n_high, lambda k: total3_copy(k).start())
    recv_inner(*gains, 0)
    fold_gains(0)
    send_inner(*owns, 0)
    local_parts(2, 6)
    recv_low(*gains2, 0)
    fold_gains2(0)
    send_high(*gains3, 0)
    recv_inner(*gains, 1)
    fold_gains(1)
    send_inner(*owns, 1)
    local_parts(6, 8)
    init_load(0).wait()
    init_load(1).wait()
    unrolled(n_high, lambda k: total3_copy(k).wait_recv())
    recv_high(*gains3, 0)
    spread_states(0)
    send_low(*befores, 0)
    recv_low(*gains2, 1)
    fold_gains2(1)
    send_high(*gains3, 1)
    recv_inner(*owns, 0)
    fold_owns(0)
    recv_low(*befores, 0)
    fill_states(0)
    send_inner(*states, 0)
    recv_high(*gains3, 1)
    spread_states(1)
    send_low(*befores, 1)
    recv_low(*owns2, 0)
    fold_owns2(0)
    send_high(*owns3, 0)
    recv_inner(*owns, 1)
    fold_owns(1)
    recv_low(*befores, 1)
    fill_states(1)
    send_inner(*states, 1)
    recv_high(*owns3, 0)
    spread_afters(0)
    send_low(*behinds, 0)
    recv_low(*owns2, 1)
    fold_owns2(1)
    send_high(*owns3, 1)
    parts(states, 0, state_part)
    recv_low(*behinds, 0)
    fill_afters(0)
    send_inner(*afters, 0)
    send_firsts(0)
    recv_high(*owns3, 1)
    spread_afters(1)
    send_low(*behinds, 1)
    parts(states, 1, state_part)
    recv_low(*behinds, 1)
    fill_afters(1)
    send_inner(*afters, 1)
    send_firsts(1)
    put_firsts(0)
    put_firsts(1)
    for half in range(2):
        unrolled(n_low, lambda k, half=half: first_copy(half, k).wait_send())
    store_start = store(0, start_ref, dstart_hbm)
    store_start.start()
    stores = [store(1, y_ref, y_hbm), store(2, dout_ref, dout_hbm)]
    for copy in stores:
        copy.start()

    unrolled(n_inner, lambda k: total_copy(k).wait_send())
    unrolled(n_low, lambda k: total2_copy(k).wait_send())
    unrolled(n_high, lambda k: total3_copy(k).wait_send())
    for half in range(2):
        for stage in (gains2, owns2, befores, behinds):
            sent_low(*stage, half)
        for stage in (gains3, owns3):
            sent_high(*stage, half)
        for stage in (gains, owns, states):
            sent_inner(*stage, half)
    row = iota((length, length), 0)
    column = iota((length, length), 1)
    up_total = exact_dot(up_sum[...], jnp.where(row >= column, 1.0, 0.0), TN)
    parts(afters, 0, after_part)
    parts(afters, 1, after_part)
    sent_inner(*afters, 0)
    sent_inner(*afters, 1)

    ddecay_ref[...] = (
        up_total
        + exact_dot(low_sum[...], jnp.where(row < column, 1.0, 0.0), TN)
        + jnp.sum(state_sum[...], axis=1, keepdims=True)
    ).astype(BF16)
    end = store(3, ddecay_ref, ddecay_hbm)
    end.start()
    for copy in [store_start] + stores + [end]:
        copy.wait()
    for half in range(2):
        for k in range(n_inner):
            for copy in part_stores(half, k):
                copy.wait()


def carry(x, decay, read_in, read_out, grad, init, n_outer, n_inner, width, depth):
    length = x.shape[0]
    groups = read_in.shape[1] // depth
    heads = decay.shape[0]
    ratio = heads // groups
    mine = heads // n_inner
    n_low = ratio
    n_high = n_outer // n_low
    vmem = pl.BlockSpec(memory_space=pltpu.VMEM)
    hbm = pl.BlockSpec(memory_space=pl.ANY)
    chunks = pltpu.VMEM((n_inner, mine * width, depth), BF16)
    runs = pltpu.VMEM((2, n_low, width, depth), BF16)
    head = pltpu.VMEM((2, width, depth), BF16)
    highs = pltpu.VMEM((2, n_high, width, depth), BF16)
    total = pltpu.VMEM((mine, depth), F32)
    wide = jax.ShapeDtypeStruct(x.shape, BF16)
    narrow = jax.ShapeDtypeStruct(read_in.shape, BF16)
    wide32 = pltpu.VMEM(x.shape, F32)
    narrow32 = pltpu.VMEM(read_in.shape, F32)
    dma = pltpu.SemaphoreType.DMA
    return pl.pallas_call(
        functools.partial(carry_kernel, n_inner, n_low, n_high, ratio, width),
        in_specs=[hbm, vmem, hbm, hbm, hbm, hbm],
        out_specs=[hbm] * 6,
        out_shape=[
            wide,
            wide,
            jax.ShapeDtypeStruct(decay.shape, BF16),
            narrow,
            narrow,
            jax.ShapeDtypeStruct((mine * width, depth), F32),
        ],
        scratch_shapes=[
            chunks,
            chunks,
            pltpu.VMEM((mine * width, depth), F32),
            wide32,
            wide32,
            pltpu.VMEM(x.shape, BF16),
            pltpu.VMEM(x.shape, BF16),
            wide32,
            wide32,
            narrow32,
            narrow32,
            pltpu.VMEM((length, heads), F32),
            pltpu.VMEM((length, heads), F32),
            pltpu.VMEM((heads, depth), F32),
            pltpu.VMEM(x.shape, BF16),
            pltpu.VMEM(x.shape, BF16),
            pltpu.VMEM(decay.shape, BF16),
            pltpu.VMEM(read_in.shape, BF16),
            pltpu.VMEM(read_out.shape, BF16),
            pltpu.VMEM(x.shape, BF16),
            pltpu.VMEM(read_in.shape, BF16),
            pltpu.VMEM(read_out.shape, BF16),
            pltpu.VMEM(grad.shape, BF16),
            pltpu.VMEM((2, width, depth), F32),
            pltpu.VMEM((n_inner, mine, depth), F32),
            pltpu.VMEM((n_inner, mine, depth), F32),
            total,
            pltpu.VMEM((n_low, mine, depth), F32),
            total,
            pltpu.VMEM((n_high, mine, depth), F32),
            chunks,
            chunks,
            chunks,
            chunks,
            runs,
            runs,
            runs,
            runs,
            head,
            highs,
            head,
            highs,
            runs,
            runs,
            runs,
            runs,
            head,
            runs,
            chunks,
            chunks,
            dma((5 + 2 * n_inner,)),
            dma((4 + 4 * n_inner,)),
            dma((9, n_inner)),
            dma((9, n_inner)),
            dma((11, n_low)),
            dma((11, n_low)),
            dma((5, n_high)),
            dma((5, n_high)),
            pltpu.SemaphoreType.REGULAR((2,)),
        ],
        compiler_params=pltpu.CompilerParams(
            collective_id=0, has_side_effects=True, vmem_limit_bytes=60 * 2**20
        ),
        name="carry",
    )(x, decay, read_in, read_out, grad, init)


def deliver_kernel(parts, *refs):
    n = len(parts)
    hbm, out, held, (loaded, stored) = refs[:n], refs[n : 2 * n], refs[2 * n : 3 * n], refs[3 * n :]
    loads, stores = [], []
    for i, part in enumerate(parts):
        rows = hbm[i].shape[0] // part
        for p in range(part):
            at, sem = pl.ds(p * rows, rows), len(loads)
            loads.append(
                pltpu.make_async_copy(hbm[i].at[at], held[i].at[at], loaded.at[sem])
            )
            stores.append(
                pltpu.make_async_copy(held[i].at[at], out[i].at[at], stored.at[sem])
            )
    for load in loads:
        load.start()
    for load, store in zip(loads, stores):
        load.wait()
        store.start()
    for store in stores:
        store.wait()


def deliver(*arrays):
    n = len(arrays)
    hbm = pl.BlockSpec(memory_space=pl.ANY)
    parts = [4 if a.size >= 2**19 else 1 for a in arrays]
    return pl.pallas_call(
        functools.partial(deliver_kernel, parts),
        in_specs=[hbm] * n,
        out_specs=[hbm] * n,
        out_shape=[jax.ShapeDtypeStruct(a.shape, a.dtype) for a in arrays],
        scratch_shapes=[pltpu.VMEM(a.shape, a.dtype) for a in arrays]
        + [pltpu.SemaphoreType.DMA((sum(parts),))] * 2,
        compiler_params=pltpu.CompilerParams(vmem_limit_bytes=60 * 2**20),
        name="deliver",
    )(*arrays)


def shards(inputs, log_decay, read_in, read_out, initial_state, output_grad):
    n_outer, n_inner = lax.axis_size("outer"), lax.axis_size("inner")
    width, depth = initial_state.shape[1:]
    decay = log_decay.T
    results = carry(
        inputs,
        decay,
        read_in,
        read_out,
        output_grad,
        initial_state.reshape(-1, depth),
        n_outer,
        n_inner,
        width,
        depth,
    )
    y, dx, ddecay, din, dout, dstart = deliver(*results)
    return (y, dx, ddecay.T, din, dout, dstart.reshape(initial_state.shape))


def solution(mesh):
    tokens = P(("outer", "inner"), None)
    held = P("inner", None, None)
    return jax.shard_map(
        shards,
        mesh=mesh,
        in_specs=(tokens, tokens, tokens, tokens, held, tokens),
        out_specs=(tokens, tokens, tokens, tokens, tokens, held),
        check_vma=False,
    )
```

```python
import functools

import jax
import jax.numpy as jnp
from jax import lax
from jax.experimental import pallas as pl
from jax.experimental.pallas import tpu as pltpu
from jax.sharding import PartitionSpec as P

F32 = jnp.float32
BF16 = jnp.bfloat16
NN = ((1,), (0,))
NT = ((1,), (1,))
TN = ((0,), (0,))
MESH = pl.DeviceIdType.MESH


def dot(a, b, dims):
    return lax.dot_general(a, b, (dims, ((), ())), preferred_element_type=F32)


def exact_dot(a, b, dims):
    return lax.dot_general(
        a, b, (dims, ((), ())), preferred_element_type=F32, precision=lax.Precision.HIGHEST
    )


def split_dot(a, b, dims):
    high = a.astype(BF16)
    low = (a - high.astype(F32)).astype(BF16)
    return dot(high, b, dims) + dot(low, b, dims)


def iota(shape, axis):
    return lax.broadcasted_iota(jnp.int32, shape, axis)


def as_bf16(mask):
    return jnp.where(mask, 1.0, 0.0).astype(BF16)


def lower(length):
    return as_bf16(iota((length, length), 0) >= iota((length, length), 1))


def spread_sums(decay_ref, group, ratio, width):
    heads, length = decay_ref.shape
    columns = ratio * width
    pick = as_bf16(iota((heads, columns), 0) == group * ratio + iota((heads, columns), 1) // width)
    return dot(lower(length), dot(decay_ref[...], pick, TN).astype(BF16), NN)


def head_decays(decay_ref, group, ratio):
    heads, length = decay_ref.shape
    pick = as_bf16(iota((ratio, heads), 1) == group * ratio + iota((ratio, heads), 0))
    return dot(pick, decay_ref[...], NN).astype(BF16)


def carry_kernel(
    n_inner,
    n_low,
    n_high,
    ratio,
    width,
    x_hbm,
    decay_ref,
    in_hbm,
    out_hbm,
    grad_hbm,
    init_hbm,
    y_hbm,
    dx_hbm,
    ddecay_hbm,
    din_hbm,
    dout_hbm,
    dstart_hbm,
    state_ref,
    after_ref,
    start_ref,
    from_start,
    to_end,
    weighted_ref,
    scaled_ref,
    y_sum,
    dx_sum,
    din_sum,
    dout_sum,
    up_sum,
    low_sum,
    state_sum,
    y_ref,
    dx_ref,
    ddecay_ref,
    din_ref,
    dout_ref,
    x_ref,
    in_ref,
    out_ref,
    grad_ref,
    init_ref,
    send_total,
    total1,
    send_total2,
    total2,
    send_total3,
    total3,
    send_gain,
    gain1,
    send_own,
    own1,
    send_gain2,
    gain2,
    send_own2,
    own2,
    send_gain3,
    gain3,
    send_own3,
    own3,
    send_before,
    before,
    send_behind,
    behind,
    send_first,
    firsts,
    send_state,
    send_after,
    load_sem,
    store_sem,
    inner_send,
    inner_recv,
    low_send,
    low_recv,
    high_send,
    high_recv,
    ready,
):
    outer = lax.axis_index("outer")
    inner = lax.axis_index("inner")
    low = lax.rem(outer, n_low)
    high = lax.div(outer, n_low)
    length = x_ref.shape[0]
    depth = in_ref.shape[1] * ratio // decay_ref.shape[0]
    columns = ratio * width

    def around(here, k, n):
        there = here + k
        return jnp.where(there >= n, there - n, there)

    def inner_peer(k):
        return around(inner, k, n_inner)

    def low_peer(k):
        return around(low, k, n_low)

    def high_peer(k):
        return around(high, k, n_high)

    def inner_id(k):
        return (outer, inner_peer(k))

    def low_id(k):
        return (high * n_low + low_peer(k), inner)

    def high_id(k):
        return (high_peer(k) * n_low + low, inner)

    def each(n, act):
        def body(k, none):
            act(k)
            return none

        lax.fori_loop(1, n, body, 0)

    def unrolled(n, act):
        for k in sorted(range(1, n), key=lambda k: -min(k, n - k)):
            act(k)

    def remote(src, dst, send, recv, to):
        return pltpu.make_async_remote_copy(
            src_ref=src,
            dst_ref=dst,
            send_sem=send,
            recv_sem=recv,
            device_id=to,
            device_id_type=MESH,
        )

    def inner_copy(stage, k, src, dst, at=slice(None)):
        return remote(
            src.at[inner_peer(k), at],
            dst.at[inner, at],
            inner_send.at[stage, k],
            inner_recv.at[stage, k],
            inner_id(k),
        )

    def low_copy(stage, k, src, dst, half):
        return remote(
            src.at[half, low_peer(k)],
            dst.at[half, low],
            low_send.at[stage, k],
            low_recv.at[stage, k],
            low_id(k),
        )

    def high_copy(stage, k, src, dst, half):
        return remote(
            src.at[half],
            dst.at[half, high],
            high_send.at[stage, k],
            high_recv.at[stage, k],
            high_id(k),
        )

    def first_copy(half, k):
        return remote(
            send_first.at[half],
            firsts.at[half, low],
            low_send.at[9 + half, k],
            low_recv.at[9 + half, k],
            low_id(k),
        )

    def total_copy(k):
        return remote(
            send_total.at[inner_peer(k)],
            total1.at[inner],
            inner_send.at[0, k],
            inner_recv.at[0, k],
            inner_id(k),
        )

    def total2_copy(k):
        return remote(
            send_total2, total2.at[low], low_send.at[0, k], low_recv.at[0, k], low_id(k)
        )

    def total3_copy(k):
        return remote(
            send_total3, total3.at[high], high_send.at[0, k], high_recv.at[0, k], high_id(k)
        )

    def group_slices(group):
        return (
            pl.ds(pl.multiple_of(group * columns, columns), columns),
            pl.ds(pl.multiple_of(group * depth, depth), depth),
        )

    ORDER = sorted(range(1, n_inner), key=lambda k: -min(k, n_inner - k))

    def x_load(half, k):
        wide = group_slices(2 * inner_peer(k) + half)[0]
        return pltpu.make_async_copy(
            x_hbm.at[:, wide], x_ref.at[:, wide], load_sem.at[5 + half * n_inner + k]
        )

    def load(i, src, dst):
        return pltpu.make_async_copy(src, dst, load_sem.at[i])

    def init_load(half):
        rows = pl.ds(pl.multiple_of((half * ratio + low) * width, width), width)
        return load(half, init_hbm.at[rows], init_ref.at[half])

    load_in, load_grad, load_out = (
        load(2, in_hbm, in_ref),
        load(3, grad_hbm, grad_ref),
        load(4, out_hbm, out_ref),
    )
    load_in.start()
    for half in range(2):
        for k in ORDER + [0]:
            x_load(half, k).start()
    load_grad.start()
    load_out.start()
    init_load(0).start()
    init_load(1).start()

    barrier = pltpu.get_barrier_semaphore()
    for n, peer in ((n_inner, inner_id), (n_low, low_id), (n_high, high_id)):
        unrolled(
            n,
            lambda k, peer=peer: pl.semaphore_signal(
                barrier, inc=1, device_id=peer(k), device_id_type=MESH
            ),
        )

    def send_totals():
        totals = dot(decay_ref[...], jnp.ones((length, send_total.shape[2]), BF16), NN)
        for e in range(n_inner):
            send_total[e] = totals[e * 2 * ratio : (e + 1) * 2 * ratio]
        unrolled(n_inner, lambda k: total_copy(k).start())
        total1[inner] = send_total[inner]

    def half_rows(half):
        return pl.ds(half * columns, columns)

    def gain_of(half, k):
        group = 2 * inner_peer(k) + half
        wide, narrow = group_slices(group)
        x_load(half, k).wait()
        summed = spread_sums(decay_ref, group, ratio, width)
        from_start[:, wide] = jnp.exp(summed)
        factor = jnp.exp(summed[length - 1 :] - summed)
        to_end[:, wide] = factor
        weighted = (x_ref[:, wide].astype(F32) * factor).astype(BF16)
        weighted_ref[:, wide] = weighted
        return dot(weighted, in_ref[:, narrow], TN).astype(BF16)

    def own_of(half, k):
        wide, narrow = group_slices(2 * inner_peer(k) + half)
        scaled = (grad_ref[:, wide].astype(F32) * from_start[:, wide]).astype(BF16)
        scaled_ref[:, wide] = scaled
        return dot(scaled, out_ref[:, narrow], TN).astype(BF16)

    def local_part(group):
        wide, narrow = group_slices(group)
        picked = head_decays(decay_ref, group, ratio)
        below = lower(length)
        down = dot(below, picked, NT)
        across = dot(picked, below, NT)
        x, grad = x_ref[:, wide], grad_ref[:, wide]
        b, c = in_ref[:, narrow], out_ref[:, narrow]
        scores = dot(c, b, NT)
        causal = iota((length, length), 0) >= iota((length, length), 1)
        ys, dxs = [], []
        dscores = jnp.zeros((length, length), F32)
        for r in range(ratio):
            gap = down[:, r : r + 1] - across[r : r + 1, :]
            decays = jnp.exp(jnp.where(causal, gap, -1e30))
            weights = (scores * decays).astype(BF16)
            at = slice(r * width, (r + 1) * width)
            ys.append(dot(weights, x[:, at], NN))
            dxs.append(dot(weights, grad[:, at], TN))
            dscores = dscores + dot(grad[:, at], x[:, at], NT) * decays
        y_sum[:, wide] = jnp.concatenate(ys, axis=1)
        dx_sum[:, wide] = jnp.concatenate(dxs, axis=1)
        dscores = dscores.astype(BF16)
        dout_sum[:, narrow] = dot(dscores, b, NN)
        din_sum[:, narrow] = dot(dscores, c, TN)

    def place(group):
        heads = decay_ref.shape[0]
        head = group * ratio + iota((columns, heads), 0) // width
        return as_bf16(iota((columns, heads), 1) == head)

    def state_part(half, k):
        owner = around(inner, n_inner - k, n_inner)
        group = 2 * owner + half
        wide, narrow = group_slices(group)
        state = state_ref[owner, half_rows(half), :]
        y = y_sum[:, wide] + dot(out_ref[:, narrow], state, NT) * from_start[:, wide]
        y_ref[:, wide] = y.astype(BF16)
        dout = dout_sum[:, narrow] + dot(scaled_ref[:, wide], state, NN)
        dout_ref[:, narrow] = dout.astype(BF16)
        change = y * grad_ref[:, wide].astype(F32) - x_ref[:, wide].astype(F32) * dx_sum[:, wide]
        up_sum[...] += split_dot(change, place(group), NN)

    def part_stores(half, k):
        wide, narrow = group_slices(2 * around(inner, n_inner - k, n_inner) + half)
        return (
            store(4 + 2 * (half * n_inner + k), dx_ref.at[:, wide], dx_hbm.at[:, wide]),
            store(5 + 2 * (half * n_inner + k), din_ref.at[:, narrow], din_hbm.at[:, narrow]),
        )

    def after_part(half, k):
        owner = around(inner, n_inner - k, n_inner)
        group = 2 * owner + half
        wide, narrow = group_slices(group)
        state = state_ref[owner, half_rows(half), :]
        after = after_ref[owner, half_rows(half), :]
        far = dot(in_ref[:, narrow], after, NT) * to_end[:, wide]
        dx_ref[:, wide] = (dx_sum[:, wide] + far).astype(BF16)
        din = din_sum[:, narrow] + dot(weighted_ref[:, wide], after, NN)
        din_ref[:, narrow] = din.astype(BF16)
        low_sum[...] += split_dot(x_ref[:, wide].astype(F32) * far, place(group), NN)
        product = state.astype(F32) * after.astype(F32)
        picked = head_decays(decay_ref, group, ratio)
        total = dot(picked, jnp.ones((length, depth), BF16), NN)
        state_sum[pl.ds(pl.multiple_of(group * ratio, ratio), ratio), :] = jnp.sum(
            product.reshape(ratio, width, depth), axis=1
        ) * jnp.exp(total)
        for copy in part_stores(half, k):
            copy.start()

    def local_parts(start, stop):
        def body(group, none):
            local_part(group)
            return none

        groups = n_inner * 2
        lax.fori_loop(start * groups // 8, stop * groups // 8, body, 0)

    def parts(stage, half, part):
        part(half, 0)
        for k in ORDER:
            inner_copy(stage[0] + half, k, stage[1], stage[2], half_rows(half)).wait_recv()
            part(half, k)

    def store(i, src, dst):
        return pltpu.make_async_copy(src, dst, store_sem.at[i])

    def fill_gain(half, k):
        send_gain[inner_peer(k), half_rows(half), :] = gain_of(half, k)

    def send_gains(half, start):
        for k in ORDER[start:]:
            fill_gain(half, k)
            inner_copy(1 + half, k, send_gain, gain1, half_rows(half)).start()
        gain1[inner, half_rows(half), :] = gain_of(half, 0)

    def fill_owns(half):
        at = half_rows(half)

        def act(k):
            send_own[inner_peer(k), at, :] = own_of(half, k)

        each(n_inner, act)
        own1[inner, at, :] = own_of(half, 0)

    def send_inner(stage, src, dst, half):
        for k in ORDER:
            inner_copy(stage + half, k, src, dst, half_rows(half)).start()

    def recv_inner(stage, src, dst, half):
        unrolled(n_inner, lambda k: inner_copy(stage + half, k, src, dst, half_rows(half)).wait_recv())

    def sent_inner(stage, src, dst, half):
        unrolled(n_inner, lambda k: inner_copy(stage + half, k, src, dst, half_rows(half)).wait_send())

    def keep_inner(src, dst, half):
        at = half_rows(half)
        dst[inner, at, :] = src[inner, at, :]

    def send_low(stage, src, dst, half):
        unrolled(n_low, lambda k: low_copy(stage + half, k, src, dst, half).start())
        dst[half, low] = src[half, low]

    def recv_low(stage, src, dst, half):
        unrolled(n_low, lambda k: low_copy(stage + half, k, src, dst, half).wait_recv())

    def sent_low(stage, src, dst, half):
        unrolled(n_low, lambda k: low_copy(stage + half, k, src, dst, half).wait_send())

    def send_high(stage, src, dst, half):
        unrolled(n_high, lambda k: high_copy(stage + half, k, src, dst, half).start())
        dst[half, high] = src[half]

    def recv_high(stage, src, dst, half):
        unrolled(n_high, lambda k: high_copy(stage + half, k, src, dst, half).wait_recv())

    def sent_high(stage, src, dst, half):
        unrolled(n_high, lambda k: high_copy(stage + half, k, src, dst, half).wait_send())

    def factor1(e, head):
        return jnp.exp(total1[e, pl.ds(head, 1), :])

    def factor2(e, half):
        return jnp.exp(total2[e, pl.ds(half * ratio + low, 1), :])

    def factor3(e, half):
        return jnp.exp(total3[e, pl.ds(half * ratio + low, 1), :])

    def head_rows(head):
        return pl.ds(pl.multiple_of(head * width, width), width)

    def fold_gains(half):
        def fold(r):
            head = half * ratio + r
            at = head_rows(head)
            value = gain1[0, at, :].astype(F32)
            for e in range(1, n_inner):
                value = factor1(e, head) * value + gain1[e, at, :].astype(F32)
            return value.astype(BF16)

        def act(k):
            send_gain2[half, low_peer(k)] = fold(low_peer(k))
            low_copy(1 + half, k, send_gain2, gain2, half).start()

        unrolled(n_low, act)
        gain2[half, low] = fold(low)

    def fold_owns(half):
        def fold(r):
            head = half * ratio + r
            at = head_rows(head)
            value = own1[n_inner - 1, at, :].astype(F32)
            for e in range(n_inner - 2, -1, -1):
                value = factor1(e, head) * value + own1[e, at, :].astype(F32)
            return value.astype(BF16)

        def act(k):
            send_own2[half, low_peer(k)] = fold(low_peer(k))
            low_copy(3 + half, k, send_own2, own2, half).start()

        unrolled(n_low, act)
        own2[half, low] = fold(low)

    def fold_gains2(half):
        value = gain2[half, 0].astype(F32)
        for e in range(1, n_low):
            value = factor2(e, half) * value + gain2[half, e].astype(F32)
        send_gain3[half] = value.astype(BF16)

    def fold_owns2(half):
        value = own2[half, n_low - 1].astype(F32)
        for e in range(n_low - 2, -1, -1):
            value = factor2(e, half) * value + own2[half, e].astype(F32)
        send_own3[half] = value.astype(BF16)

    def spread_states(half):
        value = init_ref[half]
        for e in range(n_high - 1):
            later = factor3(e, half) * value + gain3[half, e].astype(F32)
            value = jnp.where(e < high, later, value)
        for e in range(n_low):
            send_before[half, e] = value.astype(BF16)
            if e < n_low - 1:
                value = factor2(e, half) * value + gain2[half, e].astype(F32)

    def spread_afters(half):
        value = jnp.zeros(init_ref.shape[1:], F32)
        first = value
        for e in range(n_high - 1, -1, -1):
            first = factor3(e, half) * first + own3[half, e].astype(F32)
            value = jnp.where(e > high, first, value)
        send_first[half] = first.astype(BF16)
        for e in range(n_low - 1, -1, -1):
            send_behind[half, e] = value.astype(BF16)
            if e > 0:
                value = factor2(e, half) * value + own2[half, e].astype(F32)

    def fill_states(half):
        def fill(r):
            head = half * ratio + r
            at = head_rows(head)
            value = before[half, r].astype(F32)
            for e in range(n_inner):
                send_state[e, at, :] = value.astype(BF16)
                if e < n_inner - 1:
                    value = factor1(e, head) * value + gain1[e, at, :].astype(F32)

        def act(k):
            low_copy(5 + half, k, send_before, before, half).wait_recv()
            fill(around(low, n_low - k, n_low))

        fill(low)
        unrolled(n_low, act)
        keep_inner(send_state, state_ref, half)

    def fill_afters(half):
        def fill(r):
            head = half * ratio + r
            at = head_rows(head)
            value = behind[half, r].astype(F32)
            for e in range(n_inner - 1, -1, -1):
                send_after[e, at, :] = value.astype(BF16)
                if e > 0:
                    value = factor1(e, head) * value + own1[e, at, :].astype(F32)

        def act(k):
            low_copy(7 + half, k, send_behind, behind, half).wait_recv()
            fill(around(low, n_low - k, n_low))

        fill(low)
        unrolled(n_low, act)
        keep_inner(send_after, after_ref, half)

    def send_firsts(half):
        unrolled(n_low, lambda k: first_copy(half, k).start())
        firsts[half, low] = send_first[half]

    def put_firsts(half):
        unrolled(n_low, lambda k: first_copy(half, k).wait_recv())
        for r in range(ratio):
            start_ref[pl.ds((half * ratio + r) * width, width), :] = firsts[half, r].astype(F32)

    gains, owns = (1, send_gain, gain1), (3, send_own, own1)
    states, afters = (5, send_state, state_ref), (7, send_after, after_ref)
    gains2, owns2 = (1, send_gain2, gain2), (3, send_own2, own2)
    befores, behinds = (5, send_before, before), (7, send_behind, behind)
    gains3, owns3 = (1, send_gain3, gain3), (3, send_own3, own3)

    up_sum[...] = jnp.zeros_like(up_sum)
    low_sum[...] = jnp.zeros_like(low_sum)
    load_in.wait()
    fill_gain(0, ORDER[0])
    pl.semaphore_wait(barrier, n_inner + n_low + n_high - 3)
    send_totals()
    inner_copy(1, ORDER[0], send_gain, gain1, half_rows(0)).start()
    send_gains(0, 1)
    send_gains(1, 0)
    load_grad.wait()
    load_out.wait()
    fill_owns(0)

    unrolled(n_inner, lambda k: total_copy(k).wait_recv())
    row = total1[0]
    for e in range(1, n_inner):
        row = row + total1[e]
    send_total2[...] = row
    total2[low] = row
    unrolled(n_low, lambda k: total2_copy(k).start())
    fill_owns(1)
    local_parts(0, 2)

    unrolled(n_low, lambda k: total2_copy(k).wait_recv())
    row = total2[0]
    for e in range(1, n_low):
        row = row + total2[e]
    send_total3[...] = row
    total3[high] = row
    unrolled(n_high, lambda k: total3_copy(k).start())
    recv_inner(*gains, 0)
    fold_gains(0)
    send_inner(*owns, 0)
    local_parts(2, 6)
    recv_low(*gains2, 0)
    fold_gains2(0)
    send_high(*gains3, 0)
    recv_inner(*gains, 1)
    fold_gains(1)
    send_inner(*owns, 1)
    local_parts(6, 8)
    init_load(0).wait()
    init_load(1).wait()
    unrolled(n_high, lambda k: total3_copy(k).wait_recv())
    recv_high(*gains3, 0)
    spread_states(0)
    send_low(*befores, 0)
    recv_low(*gains2, 1)
    fold_gains2(1)
    send_high(*gains3, 1)
    recv_inner(*owns, 0)
    fold_owns(0)
    fill_states(0)
    send_inner(*states, 0)
    recv_high(*gains3, 1)
    spread_states(1)
    send_low(*befores, 1)
    recv_low(*owns2, 0)
    fold_owns2(0)
    send_high(*owns3, 0)
    recv_inner(*owns, 1)
    fold_owns(1)
    fill_states(1)
    send_inner(*states, 1)
    recv_high(*owns3, 0)
    spread_afters(0)
    send_low(*behinds, 0)
    recv_low(*owns2, 1)
    fold_owns2(1)
    send_high(*owns3, 1)
    parts(states, 0, state_part)
    fill_afters(0)
    send_inner(*afters, 0)
    send_firsts(0)
    recv_high(*owns3, 1)
    spread_afters(1)
    send_low(*behinds, 1)
    parts(states, 1, state_part)
    fill_afters(1)
    send_inner(*afters, 1)
    send_firsts(1)
    put_firsts(0)
    put_firsts(1)
    for half in range(2):
        unrolled(n_low, lambda k, half=half: first_copy(half, k).wait_send())
    store_start = store(0, start_ref, dstart_hbm)
    store_start.start()
    stores = [store(1, y_ref, y_hbm), store(2, dout_ref, dout_hbm)]
    for copy in stores:
        copy.start()

    unrolled(n_inner, lambda k: total_copy(k).wait_send())
    unrolled(n_low, lambda k: total2_copy(k).wait_send())
    unrolled(n_high, lambda k: total3_copy(k).wait_send())
    for half in range(2):
        for stage in (gains2, owns2, befores, behinds):
            sent_low(*stage, half)
        for stage in (gains3, owns3):
            sent_high(*stage, half)
        for stage in (gains, owns, states):
            sent_inner(*stage, half)
    row = iota((length, length), 0)
    column = iota((length, length), 1)
    up_total = exact_dot(up_sum[...], jnp.where(row >= column, 1.0, 0.0), TN)
    parts(afters, 0, after_part)
    parts(afters, 1, after_part)
    sent_inner(*afters, 0)
    sent_inner(*afters, 1)

    ddecay_ref[...] = (
        up_total
        + exact_dot(low_sum[...], jnp.where(row < column, 1.0, 0.0), TN)
        + jnp.sum(state_sum[...], axis=1, keepdims=True)
    ).astype(BF16)
    end = store(3, ddecay_ref, ddecay_hbm)
    end.start()
    for copy in [store_start] + stores + [end]:
        copy.wait()
    for half in range(2):
        for k in range(n_inner):
            for copy in part_stores(half, k):
                copy.wait()


def carry(x, decay, read_in, read_out, grad, init, n_outer, n_inner, width, depth):
    length = x.shape[0]
    groups = read_in.shape[1] // depth
    heads = decay.shape[0]
    ratio = heads // groups
    mine = heads // n_inner
    n_low = ratio
    n_high = n_outer // n_low
    vmem = pl.BlockSpec(memory_space=pltpu.VMEM)
    hbm = pl.BlockSpec(memory_space=pl.ANY)
    chunks = pltpu.VMEM((n_inner, mine * width, depth), BF16)
    runs = pltpu.VMEM((2, n_low, width, depth), BF16)
    head = pltpu.VMEM((2, width, depth), BF16)
    highs = pltpu.VMEM((2, n_high, width, depth), BF16)
    total = pltpu.VMEM((mine, depth), F32)
    wide = jax.ShapeDtypeStruct(x.shape, BF16)
    narrow = jax.ShapeDtypeStruct(read_in.shape, BF16)
    wide32 = pltpu.VMEM(x.shape, F32)
    narrow32 = pltpu.VMEM(read_in.shape, F32)
    dma = pltpu.SemaphoreType.DMA
    return pl.pallas_call(
        functools.partial(carry_kernel, n_inner, n_low, n_high, ratio, width),
        in_specs=[hbm, vmem, hbm, hbm, hbm, hbm],
        out_specs=[hbm] * 6,
        out_shape=[
            wide,
            wide,
            jax.ShapeDtypeStruct(decay.shape, BF16),
            narrow,
            narrow,
            jax.ShapeDtypeStruct((mine * width, depth), F32),
        ],
        scratch_shapes=[
            chunks,
            chunks,
            pltpu.VMEM((mine * width, depth), F32),
            wide32,
            wide32,
            pltpu.VMEM(x.shape, BF16),
            pltpu.VMEM(x.shape, BF16),
            wide32,
            wide32,
            narrow32,
            narrow32,
            pltpu.VMEM((length, heads), F32),
            pltpu.VMEM((length, heads), F32),
            pltpu.VMEM((heads, depth), F32),
            pltpu.VMEM(x.shape, BF16),
            pltpu.VMEM(x.shape, BF16),
            pltpu.VMEM(decay.shape, BF16),
            pltpu.VMEM(read_in.shape, BF16),
            pltpu.VMEM(read_out.shape, BF16),
            pltpu.VMEM(x.shape, BF16),
            pltpu.VMEM(read_in.shape, BF16),
            pltpu.VMEM(read_out.shape, BF16),
            pltpu.VMEM(grad.shape, BF16),
            pltpu.VMEM((2, width, depth), F32),
            pltpu.VMEM((n_inner, mine, depth), F32),
            pltpu.VMEM((n_inner, mine, depth), F32),
            total,
            pltpu.VMEM((n_low, mine, depth), F32),
            total,
            pltpu.VMEM((n_high, mine, depth), F32),
            chunks,
            chunks,
            chunks,
            chunks,
            runs,
            runs,
            runs,
            runs,
            head,
            highs,
            head,
            highs,
            runs,
            runs,
            runs,
            runs,
            head,
            runs,
            chunks,
            chunks,
            dma((5 + 2 * n_inner,)),
            dma((4 + 4 * n_inner,)),
            dma((9, n_inner)),
            dma((9, n_inner)),
            dma((11, n_low)),
            dma((11, n_low)),
            dma((5, n_high)),
            dma((5, n_high)),
            pltpu.SemaphoreType.REGULAR((2,)),
        ],
        compiler_params=pltpu.CompilerParams(
            collective_id=0, has_side_effects=True, vmem_limit_bytes=60 * 2**20
        ),
        name="carry",
    )(x, decay, read_in, read_out, grad, init)


def deliver_kernel(parts, *refs):
    n = len(parts)
    hbm, out, held, (loaded, stored) = refs[:n], refs[n : 2 * n], refs[2 * n : 3 * n], refs[3 * n :]
    loads, stores = [], []
    for i, part in enumerate(parts):
        rows = hbm[i].shape[0] // part
        for p in range(part):
            at, sem = pl.ds(p * rows, rows), len(loads)
            loads.append(
                pltpu.make_async_copy(hbm[i].at[at], held[i].at[at], loaded.at[sem])
            )
            stores.append(
                pltpu.make_async_copy(held[i].at[at], out[i].at[at], stored.at[sem])
            )
    for load in loads:
        load.start()
    for load, store in zip(loads, stores):
        load.wait()
        store.start()
    for store in stores:
        store.wait()


def deliver(*arrays):
    n = len(arrays)
    hbm = pl.BlockSpec(memory_space=pl.ANY)
    parts = [4 if a.size >= 2**19 else 1 for a in arrays]
    return pl.pallas_call(
        functools.partial(deliver_kernel, parts),
        in_specs=[hbm] * n,
        out_specs=[hbm] * n,
        out_shape=[jax.ShapeDtypeStruct(a.shape, a.dtype) for a in arrays],
        scratch_shapes=[pltpu.VMEM(a.shape, a.dtype) for a in arrays]
        + [pltpu.SemaphoreType.DMA((sum(parts),))] * 2,
        compiler_params=pltpu.CompilerParams(vmem_limit_bytes=60 * 2**20),
        name="deliver",
    )(*arrays)


def shards(inputs, log_decay, read_in, read_out, initial_state, output_grad):
    n_outer, n_inner = lax.axis_size("outer"), lax.axis_size("inner")
    width, depth = initial_state.shape[1:]
    decay = log_decay.T
    results = carry(
        inputs,
        decay,
        read_in,
        read_out,
        output_grad,
        initial_state.reshape(-1, depth),
        n_outer,
        n_inner,
        width,
        depth,
    )
    y, dx, ddecay, din, dout, dstart = deliver(*results)
    return (y, dx, ddecay.T, din, dout, dstart.reshape(initial_state.shape))


def solution(mesh):
    tokens = P(("outer", "inner"), None)
    held = P("inner", None, None)
    return jax.shard_map(
        shards,
        mesh=mesh,
        in_specs=(tokens, tokens, tokens, tokens, held, tokens),
        out_specs=(tokens, tokens, tokens, tokens, tokens, held),
        check_vma=False,
    )
```
